256 devices in a mesh: aux: 32 (over x, y, core), orb: 8 (over z).
Axes of the slice: x: 4, y: 4, z: 8, core: 2. Of those that a mesh axis runs over, the one named last changes fastest.
Arguments:
- three_index: bfloat16 [64, 192, 128, 128], P('aux', 'orb'), may hold values from -0.5 to 0.5
- home_panels: bfloat16 [32, 20480, 128], P('aux', 'orb')
- panel_owner: int32 [32], replicated, may hold values from 0 to 31, each once
- block_row: int32 [32, 8, 24], P('aux', 'orb'), may hold values from 0 to 19
- block_column: int32 [32, 8, 24], P('aux', 'orb'), may hold values from 0 to 159
- block_count: int32 [32, 8], P('aux', 'orb'), may hold values from 1 to 24, as said below
Outputs:
- exchange_occ: float32 [20480, 256], P('orb', 'aux')
The draws below stay inside these ranges and needn't reach their ends.
Inputs may be any that keep to these rules, and one draw needn't show every extreme that they name: `block_count`: some aux shard and row shard has all 24 slots live.
All inputs are finite; a program needn't handle non-finite values.
Results may differ from the reference program's by a relative error of at most 0.0037.
Values may be sent and summed in bfloat16 or wider, within the bound.
A program may use at most 64 MiB of HBM per device.

```python
import jax
import jax.numpy as jnp
from jax import lax

NBF = 20480
BLK = 128
PANEL = 128
PANELS = 2
AUX_DEV = 2
SLOTS = 24
AUX = 64
NOW = 256
N_AUX = 32
N_ORB = 8


def draw_home_panels(key, part):
    key = jax.random.fold_in(key, 11)
    factor = (0.3 * float(AUX * NOW) ** 0.5 * float(NBF) ** 0.5) ** (-1.0 / 3.0)
    values = jax.random.normal(key, (N_AUX, NBF, PANEL), jnp.float32)
    return (factor * values).astype(jnp.bfloat16)


def draw_block_count(key, part):
    key = jax.random.fold_in(key, 23)
    split_keys = jax.random.split(key)
    divisor = jax.random.randint(split_keys[0], (N_AUX * N_ORB,), 1, 7)
    counts = jnp.maximum(SLOTS // divisor, 1)
    chosen = jax.random.randint(split_keys[1], (), 0, N_AUX * N_ORB)
    counts = jnp.where(jnp.arange(N_AUX * N_ORB) == chosen, SLOTS, counts)
    return counts.reshape(N_AUX, N_ORB).astype(jnp.int32)


def with_ends(values, stream_key, least, largest):
    longest = values.shape.index(max(values.shape))
    spots = []
    for shift in (0, 1):
        where = [jax.random.randint(jax.random.fold_in(stream_key, axis), (), 0, length) for axis, length in enumerate(values.shape)]
        where[longest] = (where[longest] + shift) % values.shape[longest]
        spots.append(tuple(where))
    return values.at[spots[0]].set(least).at[spots[1]].set(largest)


def block_scale(rng, dims, pieces, low, largest):
    def one(axis_at, shards_of):
        heights = jax.random.uniform(jax.random.fold_in(jax.random.fold_in(rng, 6), axis_at), (shards_of,), jnp.float32, low / len(pieces), largest / len(pieces))
        return jnp.repeat(jnp.exp(heights), dims[axis_at] // shards_of).reshape((-1,) + (1,) * (len(dims) - axis_at - 1))

    loudness = one(*pieces[0])
    for cut in pieces[1:]:
        loudness = loudness * one(*cut)
    return loudness


def centred(rng, dims, spread, limit, pieces=(), kind=jnp.bfloat16):
    loudness = block_scale(rng, dims, pieces, -0.22, 0.18) if pieces else 1.0
    values = jax.random.normal(rng, dims, jnp.float32) * spread * loudness
    return jnp.minimum(jnp.maximum(values, -limit), limit).astype(kind)


def setup_inputs(seed: int = 0) -> dict:
    seeds = jax.random.split(jax.random.key(seed), 7)
    return {
        "three_index": centred(seeds[0], (AUX, N_ORB * SLOTS, BLK, BLK), BLK ** -0.5, 0.5, ((0, 32), (1, 8))),
        "home_panels": draw_home_panels(jax.random.fold_in(seeds[6], 71), 0),
        "panel_owner": jax.random.permutation(seeds[2], N_AUX).astype(jnp.int32),
        "block_row": with_ends(jax.random.randint(seeds[3], (N_AUX, N_ORB, SLOTS), 0, NBF // (BLK * N_ORB)), jax.random.fold_in(seeds[3], 1), 0, (NBF // (BLK * N_ORB)) - 1).astype(jnp.int32),
        "block_column": with_ends(jax.random.randint(seeds[4], (N_AUX, N_ORB, SLOTS), 0, NBF // BLK), jax.random.fold_in(seeds[4], 1), 0, (NBF // BLK) - 1).astype(jnp.int32),
        "block_count": draw_block_count(jax.random.fold_in(seeds[6], 71), 0),
    }


def reference(three_index, home_panels, panel_owner, block_row, block_column, block_count):
    rows_local = NBF // N_ORB
    row_blocks = rows_local // BLK
    coefficients = jnp.concatenate([home_panels[panel_owner[panel_index]] for panel_index in range(PANELS)], axis=1).astype(jnp.float32)
    tile_grid = coefficients.reshape(NBF // BLK, BLK, NOW)
    integrals = three_index.reshape(N_AUX, AUX_DEV, N_ORB, SLOTS, BLK, BLK)
    slot_ids = jnp.arange(SLOTS, dtype=jnp.int32)
    block_ids = jnp.arange(row_blocks, dtype=jnp.int32)

    def one_shard(running, inputs):
        slab_values, row_list, column_list, live_count = inputs
        slab_values = slab_values.astype(jnp.float32)
        picked = tile_grid[column_list]
        products = jnp.einsum("posmk,oskj->posmj", slab_values, picked, precision=lax.Precision.HIGHEST)
        live_mask = (slot_ids[None, :] < live_count[:, None]).astype(jnp.float32)
        placing = (row_list[:, :, None] == block_ids[None, None, :]).astype(jnp.float32) * live_mask[:, :, None]
        placed = jnp.einsum("ost,posmj->potmj", placing, products, precision=lax.Precision.HIGHEST)
        halfway = placed.reshape(AUX_DEV, NBF, NOW).astype(jnp.bfloat16)
        halfway = lax.optimization_barrier(halfway).astype(jnp.float32)
        intersection = jnp.einsum("pni,nj->pij", halfway, coefficients, precision=lax.Precision.HIGHEST).astype(jnp.bfloat16)
        intersection = lax.optimization_barrier(intersection).astype(jnp.float32)
        running = running + jnp.einsum("pmi,pij->mj", halfway, intersection, precision=lax.Precision.HIGHEST)
        return running, None

    initial = jnp.zeros((NBF, NOW), jnp.float32)
    result, unused = lax.scan(one_shard, initial, (integrals, block_row, block_column, block_count))
    return result
```

```python
import functools

import jax
import jax.numpy as jnp
from jax import lax
from jax.experimental import pallas as pl
from jax.experimental.pallas import tpu as pltpu
from jax.sharding import PartitionSpec as P

MESH = pl.DeviceIdType.MESH
BF16 = jnp.bfloat16
F32 = jnp.float32
BLK = 128
NX, NY, NZ = 4, 4, 8
CHIPS = NX * NY
PLANE = [(dx, dy) for dx in range(NX) for dy in range(NY) if (dx, dy) != (0, 0)]


def here():
    a = lax.axis_index("aux")
    return a // 8, (a // 2) % 4, a % 2, lax.axis_index("orb")


def device(x, y, core, z):
    return ((x * 4 + y) * 2 + core, z)


class Copies:
    def __init__(self, send, recv):
        self.send, self.recv, self.made = send, recv, []

    def start(self, src, dst, target):
        i = len(self.made)
        copy = pltpu.make_async_remote_copy(
            src_ref=src, dst_ref=dst, send_sem=self.send.at[i], recv_sem=self.recv.at[i],
            device_id=target, device_id_type=MESH,
        )
        copy.start()
        self.made.append(copy)
        return copy

    def drain(self):
        for copy in self.made:
            copy.wait_send()


def greet(targets):
    barrier = pltpu.get_barrier_semaphore()
    for target in targets:
        pl.semaphore_signal(barrier, inc=1, device_id=target, device_id_type=MESH)
    return barrier


def peers(x, y, c, z):
    return (
        [device((x + dx) % NX, (y + dy) % NY, c, z) for dx, dy in PLANE]
        + [device(x, y, c, (z + dz) % NZ) for dz in range(1, NZ)]
        + [device(x, y, 1 - c, z)]
    )


GATHER_COPIES = 90


def gather_kernel(owner, home, tri, row, col, cnt, c_out, cl, tri_o, row_o, col_o, cnt_o,
                  land, sel, cand, mine, send, recv, local):
    x, y, c, z = here()
    chip = x * 4 + y
    other = device(x, y, 1 - c, z)
    targets = peers(x, y, c, z)
    barrier = greet(targets)
    keep = pltpu.make_async_copy(home.at[chip], land.at[chip], local.at[0])
    keep.start()
    pl.semaphore_wait(barrier, len(targets))
    net = Copies(send, recv)

    scatter = []
    for dx, dy in PLANE:
        to = ((x + dx) % NX) * 4 + (y + dy) % NY
        scatter.append(net.start(home.at[to], land.at[chip], device((x + dx) % NX, (y + dy) % NY, c, z)))
    swaps = [net.start(tri, tri_o, other), net.start(row, row_o, other), net.start(col, col_o, other),
             net.start(cnt, cnt_o, other)]
    keep.wait()
    for copy in scatter:
        copy.wait_recv()
    sel[...] = land[owner[1 - c] // 2]
    passed = net.start(sel, cand.at[1], other)
    cand[0] = land[owner[c] // 2]
    passed.wait_recv()
    mine[...] = cand[(owner[c] + c) % 2]

    keep = pltpu.make_async_copy(mine, c_out.at[z, chip], local.at[1])
    keep.start()
    column = [net.start(mine, c_out.at[z, chip], device(x, y, c, (z + dz) % NZ)) for dz in range(1, NZ)]
    keep.wait()
    for copy in column:
        copy.wait_recv()

    def piece(h, u, v, first, n):
        u, v = u % 4, v % 4
        return c_out.at[pl.ds(h * 4 + first, n), u * 4 + v if h == 0 else v * 4 + u]

    def at(h, u, v):
        u, v = u % 4, v % 4
        return device(u, v, c, z) if h == 0 else device(v, u, c, z)

    def push(h, src, u, v):
        return net.start(src, src, at(h, u, v))

    uv = [(x, y), (y, x)]
    chunks = {}

    def spread(h, q, du):
        u, v = uv[h]
        src = piece(h, u + du, v, 0, 4)
        chunks[h, q] = [push(h, src, u, v + 1), push(h, src, u, v + 3)]

    def relay(h, q, du):
        u, v = uv[h]
        up, down = chunks[h, q]
        up.wait_recv()
        a = push(h, piece(h, u + du, v + 3, 0, 2), u, v + 1)
        down.wait_recv()
        b = push(h, piece(h, u + du, v + 1, 2, 2), u, v + 3)
        tail.extend([a, b])

    tail = []
    first = {}
    for h in range(2):
        u, v = uv[h]
        src = piece(h, u, v, 0, 4)
        first[h] = [push(h, src, u + 1, v), push(h, src, u + 3, v)]
    for h in range(2):
        spread(h, 0, 0)
    second = {}
    for h in range(2):
        u, v = uv[h]
        first[h][0].wait_recv()
        a = push(h, piece(h, u + 3, v, 0, 2), u + 1, v)
        first[h][1].wait_recv()
        b = push(h, piece(h, u + 1, v, 2, 2), u + 3, v)
        second[h] = [a, b]
        spread(h, 1, 3)
        spread(h, 2, 1)
    for h in range(2):
        relay(h, 0, 0)
    for h in range(2):
        for copy in second[h]:
            copy.wait_recv()
        spread(h, 3, 2)
    for q, du in ((1, 3), (2, 1), (3, 2)):
        for h in range(2):
            relay(h, q, du)
    for copy in tail:
        copy.wait_recv()

    keep = pltpu.make_async_copy(c_out.at[z], cl.at[0], local.at[2])
    keep.start()
    swaps.append(net.start(c_out.at[z], cl.at[1], other))
    keep.wait()
    for copy in swaps:
        copy.wait_recv()
    net.drain()


def half_kernel(row, col, cnt, row_o, col_o, cnt_o, tri, tri_o, blocks, out, cbuf, tbuf, acc, csem, tsem):
    slots = tri.shape[1]
    lists = ((row, col, cnt, tri), (row_o, col_o, cnt_o, tri_o))

    def copies(u, s):
        _, cl, _, t = lists[u]
        return (
            pltpu.make_async_copy(blocks.at[cl[0, 0, s]], cbuf.at[u * slots + s], csem.at[u * slots + s]),
            pltpu.make_async_copy(t.at[:, s], tbuf.at[u * slots + s], tsem.at[u * slots + s]),
        )

    for u in range(2):
        @pl.loop(0, lists[u][2][0, 0])
        def _(s, u=u):
            for copy in copies(u, s):
                copy.start()

    acc[...] = jnp.zeros_like(acc)
    for u in range(2):
        @pl.loop(0, lists[u][2][0, 0])
        def _(s, u=u):
            for copy in copies(u, s):
                copy.wait()
            t = tbuf[u * slots + s].reshape(2 * BLK, BLK)
            prod = lax.dot_general(cbuf[u * slots + s], t, (((0,), (1,)), ((), ())), preferred_element_type=F32)
            at = pl.ds(pl.multiple_of(lists[u][0][0, 0, s] * BLK, BLK), BLK)
            acc[2 * u * BLK:(2 * u + 1) * BLK, at] += prod[:, :BLK]
            acc[(2 * u + 1) * BLK:(2 * u + 2) * BLK, at] += prod[:, BLK:]
    out[...] = acc[...].astype(BF16)


def exchange_kernel(ht, cl, out, ip, rs_land, ifull, itf, eown, eoth, eland, ssend, sland, send, recv):
    x, y, c, z = here()
    other = device(x, y, 1 - c, z)
    targets = peers(x, y, c, z)
    barrier = greet(targets)
    net = Copies(send, recv)
    rows = ht.shape[1]
    tiles = rows // 256

    for j in range(2):
        part = jnp.dot(ht[...], cl[j], preferred_element_type=F32)
        ip[:, :, j * BLK:(j + 1) * BLK] = part.astype(BF16).reshape(NZ, -1, BLK)
    pl.semaphore_wait(barrier, len(targets))
    shares = []
    for dz in range(1, NZ):
        to = (z + dz) % NZ
        shares.append(net.start(ip.at[to], rs_land.at[dz], device(x, y, c, to)))
    total = ip[z].astype(F32)
    for dz in range(1, NZ):
        shares[dz - 1].wait_recv()
        total += rs_land[dz].astype(F32)
    ifull[z] = total.astype(BF16)
    shares = [net.start(ifull.at[z], ifull.at[z], device(x, y, c, (z + dz) % NZ)) for dz in range(1, NZ)]
    for copy in shares:
        copy.wait_recv()

    width = ifull.shape[2]
    inner = ht.shape[0]
    itf[...] = ifull[...].reshape(inner, width).astype(F32).T.reshape(CHIPS, 2, 8, inner)
    it = jnp.concatenate([itf[:, 1 - c].reshape(-1, inner), itf[:, c].reshape(-1, inner)], axis=0).astype(BF16)
    swaps = []
    for t in range(tiles):
        e = jnp.dot(it, ht[:, t * 256:(t + 1) * 256], preferred_element_type=F32)
        e = e.reshape(2, CHIPS, 8, 256)
        e = jnp.concatenate([e[..., :BLK], e[..., BLK:]], axis=2)
        eoth[:, :, t * BLK:(t + 1) * BLK] = e[0].astype(BF16)
        eown[:, :, t * BLK:(t + 1) * BLK] = e[1]
        if t + 1 in (tiles // 2, tiles):
            part = pl.ds((t + 1 - tiles // 2) * BLK, tiles // 2 * BLK)
            swaps.append(net.start(eoth.at[:, :, part], eland.at[:, :, part], other))
    for copy in swaps:
        copy.wait_recv()
    for d in range(CHIPS):
        summed = eown[d] + eland[(d + 8) % CHIPS].astype(F32)
        eown[d] = summed
        ssend[d] = summed.astype(BF16)
    shares = []
    for i, (dx, dy) in enumerate(PLANE):
        to = ((x + dx) % NX) * 4 + (y + dy) % NY
        shares.append(net.start(ssend.at[(to + 8 * c) % CHIPS], sland.at[i],
                                device((x + dx) % NX, (y + dy) % NY, c, z)))
    eown[0] = eown[(x * 4 + y + 8 * c) % CHIPS]
    for i, copy in enumerate(shares):
        copy.wait_recv()
        eown[0] += sland[i].astype(F32)
    for t in range(tiles):
        out[:, t * 256:t * 256 + BLK] = eown[0, 0:8, t * BLK:(t + 1) * BLK]
        out[:, t * 256 + BLK:(t + 1) * 256] = eown[0, 8:16, t * BLK:(t + 1) * BLK]
    net.drain()


def body(three_index, home_panels, panel_owner, block_row, block_column, block_count):
    aux_local, slots = three_index.shape[:2]
    rows, width = home_panels.shape[1:]
    cut = rows // CHIPS
    anywhere = pl.BlockSpec(memory_space=pl.ANY)
    smem = pl.BlockSpec(memory_space=pltpu.SMEM)
    vmem = pl.BlockSpec(memory_space=pltpu.VMEM)
    shape = jax.ShapeDtypeStruct
    dma = pltpu.SemaphoreType.DMA

    panel, local_rows, tri_o, row_o, col_o, cnt_o = pl.pallas_call(
        gather_kernel,
        name="gather",
        out_shape=[
            shape((NZ, CHIPS, cut, width), BF16),
            shape((2, CHIPS, cut, width), BF16),
            shape(three_index.shape, BF16),
            shape(block_row.shape, jnp.int32),
            shape(block_column.shape, jnp.int32),
            shape(block_count.shape, jnp.int32),
        ],
        in_specs=[smem] + [anywhere] * 5,
        out_specs=[anywhere] * 6,
        scratch_shapes=[
            pltpu.VMEM((CHIPS, cut, width), BF16),
            pltpu.VMEM((cut, width), BF16),
            pltpu.VMEM((2, cut, width), BF16),
            pltpu.VMEM((cut, width), BF16),
            dma((GATHER_COPIES,)),
            dma((GATHER_COPIES,)),
            dma((3,)),
        ],
        compiler_params=pltpu.CompilerParams(collective_id=0, has_side_effects=True, vmem_limit_bytes=48 * 2**20),
    )(panel_owner, home_panels.reshape(CHIPS, cut, width), three_index, block_row, block_column, block_count)

    inner = 2 * aux_local * width
    halfway = pl.pallas_call(
        half_kernel,
        name="halfway",
        out_shape=shape((inner, rows), BF16),
        in_specs=[smem] * 6 + [anywhere] * 3,
        out_specs=vmem,
        scratch_shapes=[
            pltpu.VMEM((2 * slots, BLK, width), BF16),
            pltpu.VMEM((2 * slots, aux_local, BLK, BLK), BF16),
            pltpu.VMEM((inner, rows), F32),
            dma((2 * slots,)),
            dma((2 * slots,)),
        ],
        compiler_params=pltpu.CompilerParams(vmem_limit_bytes=48 * 2**20),
    )(block_row, block_column, block_count, row_o, col_o, cnt_o, three_index, tri_o,
      panel.reshape(-1, BLK, width))

    now = 2 * width
    packed = (CHIPS, 16, rows // 2)
    out = pl.pallas_call(
        exchange_kernel,
        name="exchange",
        out_shape=shape((8, rows), F32),
        in_specs=[vmem, vmem],
        out_specs=vmem,
        scratch_shapes=[
            pltpu.VMEM((NZ, inner // NZ, now), BF16),
            pltpu.VMEM((NZ, inner // NZ, now), BF16),
            pltpu.VMEM((NZ, inner // NZ, now), BF16),
            pltpu.VMEM((CHIPS, 2, 8, inner), F32),
            pltpu.VMEM(packed, F32),
            pltpu.VMEM(packed, BF16),
            pltpu.VMEM(packed, BF16),
            pltpu.VMEM(packed, BF16),
            pltpu.VMEM((CHIPS - 1,) + packed[1:], BF16),
            dma((31,)),
            dma((31,)),
        ],
        compiler_params=pltpu.CompilerParams(collective_id=1, has_side_effects=True, vmem_limit_bytes=48 * 2**20),
    )(halfway, local_rows.reshape(2, rows, width))
    return out.T


def solution(mesh):
    placed = (
        P("aux", "orb", None, None),
        P("aux", "orb", None),
        P(),
        P("aux", "orb", None),
        P("aux", "orb", None),
        P("aux", "orb"),
    )
    return jax.shard_map(
        body, mesh=mesh, in_specs=placed, out_specs=P("orb", "aux"), check_vma=False
    )
```

```python
import functools

import jax
import jax.numpy as jnp
from jax import lax
from jax.experimental import pallas as pl
from jax.experimental.pallas import tpu as pltpu
from jax.sharding import PartitionSpec as P

MESH = pl.DeviceIdType.MESH
BF16 = jnp.bfloat16
F32 = jnp.float32
BLK = 128
NX, NY, NZ = 4, 4, 8
CHIPS = NX * NY
PLANE = [(dx, dy) for dx in range(NX) for dy in range(NY) if (dx, dy) != (0, 0)]
ROWS = 2560
SLOTS = 24
ROW_BLOCKS = ROWS // BLK
RING = 8
LAST = ROW_BLOCKS - RING
INNER = 512
TILE = 256
TILES = ROWS // TILE
PARTS = 2
COPIES = 180


def here():
    a = lax.axis_index("aux")
    return a // 8, (a // 2) % 4, a % 2, lax.axis_index("orb")


def device(x, y, core, z):
    return ((x * 4 + y) * 2 + core, z)


class Copies:
    def __init__(self, send, recv):
        self.send, self.recv, self.made = send, recv, []

    def start(self, src, dst, target):
        i = len(self.made)
        copy = pltpu.make_async_remote_copy(
            src_ref=src, dst_ref=dst, send_sem=self.send.at[i], recv_sem=self.recv.at[i],
            device_id=target, device_id_type=MESH,
        )
        copy.start()
        self.made.append(copy)
        return copy

    def drain(self):
        for copy in self.made:
            copy.wait_send()


def peers(x, y, c, z):
    return (
        [device((x + dx) % NX, (y + dy) % NY, c, z) for dx, dy in PLANE]
        + [device(x, y, c, (z + dz) % NZ) for dz in range(1, NZ)]
        + [device(x, y, 1 - c, z)]
    )


def wait(copies):
    for copy in copies:
        copy.wait_recv()


def kernel(owner, home, tri, row, col, cnt, out,
           panel, land0, land1, sel0, sel1, cand0, cand1, own_t, other_t, lists_v, cnt_v, row_s, col_s, cnt_s, prev, last, run, half,
           other_rows, ip, ip_land, ifull, itf, eown, eoth, eland, ssend, sland, send, recv, local):
    land, sel, cand = (land0, land1), (sel0, sel1), (cand0, cand1)
    x, y, c, z = here()
    chip = x * 4 + y
    other = device(x, y, 1 - c, z)
    targets = peers(x, y, c, z)
    barrier = pltpu.get_barrier_semaphore()
    for target in targets:
        pl.semaphore_signal(barrier, inc=1, device_id=target, device_id_type=MESH)
    net = Copies(send, recv)

    def piece(p, j):
        if p == 0:
            return pl.ds(j // 2, 1), pl.ds(j % 2 * 64, 64)
        return pl.ds(RING + j // 4 * (LAST // 4), LAST // 4), pl.ds(j % 4 * 32, 32)

    here_copies = [
        pltpu.make_async_copy(home.at[piece(0, chip)], land[0].at[chip], local.at[0]),
        pltpu.make_async_copy(home.at[piece(1, chip)], land[1].at[chip], local.at[1]),
        pltpu.make_async_copy(row, row_s.at[0], local.at[2]),
        pltpu.make_async_copy(col, col_s.at[0], local.at[3]),
        pltpu.make_async_copy(cnt, cnt_s.at[0], local.at[4]),
        pltpu.make_async_copy(tri, own_t, local.at[5]),
    ]
    for copy in here_copies:
        copy.start()
    pl.semaphore_wait(barrier, len(targets))

    scatter = []
    for p in range(2):
        scatter.append([])
        for dx, dy in PLANE:
            tx, ty = (x + dx) % NX, (y + dy) % NY
            scatter[p].append(net.start(
                home.at[piece(p, tx * 4 + ty)], land[p].at[chip], device(tx, ty, c, z)))
        if p == 0:
            row_copy = net.start(row, lists_v.at[0], other)
            col_copy = net.start(col, lists_v.at[1], other)
            cnt_copy = net.start(cnt, cnt_v, other)
    tri_copy = net.start(tri, other_t, other)

    wait([row_copy, col_copy, cnt_copy])
    to_smem = [
        pltpu.make_async_copy(lists_v.at[0], row_s.at[1], local.at[6]),
        pltpu.make_async_copy(lists_v.at[1], col_s.at[1], local.at[7]),
        pltpu.make_async_copy(cnt_v, cnt_s.at[1], local.at[8]),
    ]
    for copy in to_smem:
        copy.start()
    for copy in here_copies[2:5] + to_smem:
        copy.wait()
    for u in range(2):
        @pl.loop(0, SLOTS)
        def _(s, u=u):
            mine = row_s[u, 0, 0, s]
            found = jnp.int32(SLOTS)
            for e in range(SLOTS - 1):
                same = jnp.logical_and(row_s[u, 0, 0, e] == mine, e < s)
                found = jnp.where(same, jnp.int32(e), found)
            prev[u, s] = found

        @pl.loop(0, ROW_BLOCKS)
        def _(t, u=u):
            found = jnp.int32(SLOTS)
            for e in range(SLOTS):
                same = jnp.logical_and(row_s[u, 0, 0, e] == t, e < cnt_s[u, 0, 0])
                found = jnp.where(same, jnp.int32(e), found)
            last[u, t] = found

        run[u, SLOTS] = jnp.zeros((2 * BLK, BLK), F32)

    def choose(p):
        here_copies[p].wait()
        wait(scatter[p])
        sel[p][...] = land[p][owner[1 - c] // 2]
        passed = net.start(sel[p], cand[p].at[1], other)
        cand[p][0] = land[p][owner[c] // 2]
        passed.wait_recv()
        panel[(z,) + piece(p, chip)] = cand[p][(owner[c] + c) % 2]

    choose(0)
    mine = panel.at[(z,) + piece(0, chip)]
    plane = [net.start(mine, mine, device((x + dx) % NX, (y + dy) % NY, c, z)) for dx, dy in PLANE]
    choose(1)
    mine = panel.at[(z,) + piece(1, chip)]
    column = [net.start(mine, mine, device(x, y, c, (z + dz) % NZ)) for dz in range(1, NZ)]

    ring = {}

    def step(k, e):
        for sign in (1, -1):
            far = 4 if (sign == 1) == (e == 0) else 3
            if k > far:
                continue
            if k > 1:
                ring[k - 1, e, sign].wait_recv()
            at = (z - sign * (k - 1)) % NZ
            src = panel.at[at, pl.ds(e * (RING // 2), RING // 2)]
            ring[k, e, sign] = net.start(src, src, device(x, y, c, (z + sign) % NZ))

    wait(plane)
    step(1, 0)
    step(1, 1)
    swaps = [net.start(panel.at[z, pl.ds(0, RING)], other_rows.at[pl.ds(0, RING)], other)]

    def block(h, u, v, first, n):
        u, v = u % 4, v % 4
        return panel.at[(pl.ds(h * 4 + first, n),) + piece(1, u * 4 + v if h == 0 else v * 4 + u)]

    def push(h, src, u, v):
        u, v = u % 4, v % 4
        return net.start(src, src, device(u, v, c, z) if h == 0 else device(v, u, c, z))

    uv = [(x, y), (y, x)]
    chunks, first, second, tail = {}, {}, {}, []

    def spread(h, q, du):
        u, v = uv[h]
        src = block(h, u + du, v, 0, 4)
        chunks[h, q] = [push(h, src, u, v + 1), push(h, src, u, v + 3)]

    def relay(h, q, du):
        u, v = uv[h]
        up, down = chunks[h, q]
        up.wait_recv()
        tail.append(push(h, block(h, u + du, v + 3, 0, 2), u, v + 1))
        down.wait_recv()
        tail.append(push(h, block(h, u + du, v + 1, 2, 2), u, v + 3))

    wait(column)
    for h in range(2):
        u, v = uv[h]
        src = block(h, u, v, 0, 4)
        first[h] = [push(h, src, u + 1, v), push(h, src, u + 3, v)]
    for h in range(2):
        spread(h, 0, 0)
    step(2, 0)
    for h in range(2):
        u, v = uv[h]
        first[h][0].wait_recv()
        second[h] = [push(h, block(h, u + 3, v, 0, 2), u + 1, v)]
        first[h][1].wait_recv()
        second[h].append(push(h, block(h, u + 1, v, 2, 2), u + 3, v))
        spread(h, 1, 3)
        spread(h, 2, 1)
    step(2, 1)
    for h in range(2):
        relay(h, 0, 0)
    step(3, 0)
    for h in range(2):
        wait(second[h])
        spread(h, 3, 2)
    for h in range(2):
        relay(h, 1, 3)
    step(3, 1)
    for h in range(2):
        relay(h, 2, 1)
    step(4, 0)
    step(4, 1)
    for h in range(2):
        relay(h, 3, 2)
    wait(tail)
    swaps.append(net.start(panel.at[z, pl.ds(RING, LAST)], other_rows.at[pl.ds(RING, LAST)], other))
    wait([ring[3, 0, -1], ring[3, 1, 1], ring[4, 0, 1], ring[4, 1, -1]])

    here_copies[5].wait()
    tri_copy.wait_recv()
    for u, integrals in enumerate((own_t, other_t)):
        @pl.loop(0, SLOTS, step=2)
        def _(s0, u=u, integrals=integrals):
            products = []
            for i in range(2):
                b = col_s[u, 0, 0, s0 + i]
                rows = panel[b // ROW_BLOCKS, b % ROW_BLOCKS]
                t = integrals[:, s0 + i].reshape(2 * BLK, BLK)
                products.append(jnp.dot(t, rows, preferred_element_type=F32))
            for i in range(2):
                run[u, s0 + i] = products[i] + run[u, prev[u, s0 + i]]
    for u in range(2):
        @pl.loop(0, ROW_BLOCKS)
        def _(t, u=u):
            total = run[u, last[u, t]].astype(BF16)
            at = pl.ds(pl.multiple_of(t * BLK, BLK), BLK)
            for p in range(2):
                half[at, pl.ds((2 * u + p) * BLK, BLK)] = total[p * BLK:(p + 1) * BLK]

    wait(swaps)
    for j in range(2):
        rows = (panel[z] if j == 0 else other_rows[...]).reshape(ROWS, BLK)
        part = lax.dot_general(rows, half[...], (((0,), (0,)), ((), ())), preferred_element_type=F32)
        ip[j * 4:(j + 1) * 4] = part.astype(BF16).reshape(4, 32, INNER)
    shares = []
    for dz in range(1, NZ):
        to = (z + dz) % NZ
        shares.append(net.start(ip.at[to], ip_land.at[dz - 1], device(x, y, c, to)))
    total = ip[z].astype(F32)
    for dz in range(1, NZ):
        shares[dz - 1].wait_recv()
        total += ip_land[dz - 1].astype(F32)
    ifull[z] = total.astype(BF16)
    wait([net.start(ifull.at[z], ifull.at[z], device(x, y, c, (z + dz) % NZ)) for dz in range(1, NZ)])

    itf[...] = ifull[...].astype(F32).reshape(CHIPS, 2, 8, INNER)
    it = jnp.concatenate([itf[:, 1 - c].reshape(-1, INNER), itf[:, c].reshape(-1, INNER)], axis=0).astype(BF16)
    per = TILES // PARTS
    swaps = []
    for t in range(TILES):
        e = lax.dot_general(it, half[t * TILE:(t + 1) * TILE, :], (((1,), (1,)), ((), ())),
                            preferred_element_type=F32)
        e = e.reshape(2, CHIPS, 8, TILE)
        e = jnp.concatenate([e[..., :BLK], e[..., BLK:]], axis=2)
        eoth[t // per, :, :, t % per * BLK:(t % per + 1) * BLK] = e[0].astype(BF16)
        eown[t // per, :, :, t % per * BLK:(t % per + 1) * BLK] = e[1]
        if (t + 1) % per == 0:
            swaps.append(net.start(eoth.at[t // per], eland.at[t // per], other))
    shares = []
    for k in range(PARTS):
        swaps[k].wait_recv()
        for d in range(CHIPS):
            summed = eown[k, d] + eland[k, (d + 8) % CHIPS].astype(F32)
            eown[k, d] = summed
            ssend[k, d] = summed.astype(BF16)
        shares.append([])
        for i, (dx, dy) in enumerate(PLANE):
            tx, ty = (x + dx) % NX, (y + dy) % NY
            shares[k].append(net.start(ssend.at[k, (tx * 4 + ty + 8 * c) % CHIPS], sland.at[k, i],
                                       device(tx, ty, c, z)))
    for k in range(PARTS):
        total = eown[k, (chip + 8 * c) % CHIPS]
        for i, copy in enumerate(shares[k]):
            copy.wait_recv()
            total += sland[k, i].astype(F32)
        for t in range(per):
            at = (k * per + t) * TILE
            out[:, at:at + BLK] = total[0:8, t * BLK:(t + 1) * BLK]
            out[:, at + BLK:at + TILE] = total[8:16, t * BLK:(t + 1) * BLK]
    net.drain()


def body(three_index, home_panels, panel_owner, block_row, block_column, block_count):
    anywhere = pl.BlockSpec(memory_space=pl.ANY)
    smem = pl.BlockSpec(memory_space=pltpu.SMEM)
    dma = pltpu.SemaphoreType.DMA
    vm = pltpu.VMEM
    pieces = (1, 64, BLK), (LAST // 4, 32, BLK)
    packed = (PARTS, CHIPS, 16, ROWS // 2 // PARTS)
    out = pl.pallas_call(
        kernel,
        name="exchange",
        out_shape=jax.ShapeDtypeStruct((8, ROWS), F32),
        in_specs=[smem] + [anywhere] * 5,
        out_specs=pl.BlockSpec(memory_space=vm),
        scratch_shapes=[
            vm((NZ, ROW_BLOCKS, BLK, BLK), BF16),
            vm((CHIPS,) + pieces[0], BF16),
            vm((CHIPS,) + pieces[1], BF16),
            vm(pieces[0], BF16),
            vm(pieces[1], BF16),
            vm((2,) + pieces[0], BF16),
            vm((2,) + pieces[1], BF16),
            vm(three_index.shape, BF16),
            vm(three_index.shape, BF16),
            vm((2,) + block_row.shape, jnp.int32),
            vm(block_count.shape, jnp.int32),
            pltpu.SMEM((2,) + block_row.shape, jnp.int32),
            pltpu.SMEM((2,) + block_row.shape, jnp.int32),
            pltpu.SMEM((2,) + block_count.shape, jnp.int32),
            pltpu.SMEM((2, SLOTS), jnp.int32),
            pltpu.SMEM((2, ROW_BLOCKS), jnp.int32),
            vm((2, SLOTS + 1, 2 * BLK, BLK), F32),
            vm((ROWS, INNER), BF16),
            vm((ROW_BLOCKS, BLK, BLK), BF16),
            vm((NZ, 32, INNER), BF16),
            vm((NZ - 1, 32, INNER), BF16),
            vm((NZ, 32, INNER), BF16),
            vm((CHIPS, 2, 8, INNER), F32),
            vm(packed, F32),
            vm(packed, BF16),
            vm(packed, BF16),
            vm(packed, BF16),
            vm((PARTS, CHIPS - 1) + packed[2:], BF16),
            dma((COPIES,)),
            dma((COPIES,)),
            dma((9,)),
        ],
        compiler_params=pltpu.CompilerParams(collective_id=0, has_side_effects=True, vmem_limit_bytes=60 * 2**20),
    )(panel_owner, home_panels.reshape(ROW_BLOCKS, BLK, BLK), three_index, block_row, block_column, block_count)
    return out.T


def solution(mesh):
    placed = (
        P("aux", "orb", None, None),
        P("aux", "orb", None),
        P(),
        P("aux", "orb", None),
        P("aux", "orb", None),
        P("aux", "orb"),
    )
    return jax.shard_map(
        body, mesh=mesh, in_specs=placed, out_specs=P("orb", "aux"), check_vma=False
    )
```

```python
import math

import jax
import jax.numpy as jnp
from jax import lax
from jax.experimental import pallas as pl
from jax.experimental.pallas import tpu as pltpu
from jax.sharding import PartitionSpec as P

MESH = pl.DeviceIdType.MESH
BF16 = jnp.bfloat16
F32 = jnp.float32
BLK = 128
NX, NY, NZ = 4, 4, 8
CHIPS = NX * NY
PLANE = [(dx, dy) for dx in range(NX) for dy in range(NY) if (dx, dy) != (0, 0)]
ROWS = 2560
SLOTS = 24
ROW_BLOCKS = ROWS // BLK
BLOCKS = [4, 4, 6, 6]
FIRST = [sum(BLOCKS[:p]) for p in range(4)]
INNER = 512
TILE = 256
TILES = ROWS // TILE
PARTS = 2
UNIT = 16 * BLK
GROUPS = 99
PHASES = 7


def here():
    a = lax.axis_index("aux")
    return a // 8, (a // 2) % 4, a % 2, lax.axis_index("orb")


def device(x, y, core, z):
    return ((x * 4 + y) * 2 + core, z)


class Copies:
    def __init__(self, send, recv, ruler):
        self.send, self.recv, self.ruler = send, recv, ruler
        self.used, self.phase, self.out, self.due = 0, 0, {}, {}

    def group(self):
        self.used += 1
        return self.used - 1

    def start(self, src, dst, target, group=None, phase=None):
        group = self.group() if group is None else group
        phase = self.phase if phase is None else phase
        copy = pltpu.make_async_remote_copy(
            src_ref=src, dst_ref=dst, send_sem=self.send.at[phase], recv_sem=self.recv.at[group],
            device_id=target, device_id_type=MESH,
        )
        copy.start()
        size = math.prod(src.shape) // UNIT
        self.out[phase] = self.out.get(phase, 0) + size
        self.due[group] = self.due.get(group, 0) + size
        return group

    def take(self, sem, size):
        fits = [(a, r) for a in range(1, NZ + 1) for r in range(1, 9)
                if size % (a * r) == 0 and size // (a * r) <= ROW_BLOCKS]
        a, r = fits[0]
        ref = self.ruler.at[pl.ds(0, a), pl.ds(0, size // (a * r)), pl.ds(0, r * 16)]
        pltpu.make_async_copy(ref, ref, sem).wait()

    def wait(self, groups):
        for group in groups:
            self.take(self.recv.at[group], self.due.pop(group))

    def drain(self):
        for phase, size in self.out.items():
            self.take(self.send.at[phase], size)
        self.out = {}


def peers(x, y, c, z):
    return (
        [device((x + dx) % NX, (y + dy) % NY, c, z) for dx, dy in PLANE]
        + [device(x, y, c, (z + dz) % NZ) for dz in range(1, NZ)]
        + [device(x, y, 1 - c, z)]
    )


def kernel(owner, home, tri, row, col, cnt, out,
           panel, home_v, land0, land1, land2, land3, sel0, sel1, sel2, sel3, cand0, cand1, cand2, cand3, own_t, other_t, lists_v, cnt_v, row_s, col_s, cnt_s, prev, last, run, half,
           other_rows, ip, ip_land, ifull, eown, eoth, eland, ssend, sland, send, recv, local):
    land, sel, cand = (land0, land1, land2, land3), (sel0, sel1, sel2, sel3), (cand0, cand1, cand2, cand3)
    x, y, c, z = here()
    chip = x * 4 + y
    other = device(x, y, 1 - c, z)
    targets = peers(x, y, c, z)
    barrier = pltpu.get_barrier_semaphore()
    for target in targets:
        pl.semaphore_signal(barrier, inc=1, device_id=target, device_id_type=MESH)
    net = Copies(send, recv, panel)
    wait = net.wait

    def piece(p, j):
        n = BLOCKS[p] // 2
        return pl.ds(FIRST[p] + j // 8 * n, n), pl.ds(j % 8 * 16, 16)

    fetch = pltpu.make_async_copy(home, home_v, local.at[0])
    fetch.start()
    here_copies = [
        pltpu.make_async_copy(row, row_s.at[0], local.at[1]),
        pltpu.make_async_copy(col, col_s.at[0], local.at[2]),
        pltpu.make_async_copy(cnt, cnt_s.at[0], local.at[3]),
        pltpu.make_async_copy(tri, own_t, local.at[4]),
    ]
    for copy in here_copies[:3]:
        copy.start()
    fetch.wait()
    for p in range(4):
        land[p][chip] = home_v[piece(p, chip)]
    pl.semaphore_wait(barrier, len(targets))

    scatter = [net.group() for _ in range(4)]

    def deal(p):
        for dx, dy in PLANE:
            tx, ty = (x + dx) % NX, (y + dy) % NY
            net.start(home_v.at[piece(p, tx * 4 + ty)], land[p].at[chip], device(tx, ty, c, z), scatter[p])

    for p in range(4):
        deal(p)
    lists = [
        pltpu.make_async_remote_copy(
            src_ref=src, dst_ref=dst, send_sem=send.at[PHASES + i], recv_sem=recv.at[net.group()],
            device_id=other, device_id_type=MESH,
        )
        for i, (src, dst) in enumerate(((row, lists_v.at[0]), (col, lists_v.at[1]), (cnt, cnt_v)))
    ]
    for copy in lists:
        copy.start()
    here_copies[3].start()

    def look_up(u):
        if u == 0:
            for copy in lists:
                copy.wait()
            to_smem = [
                pltpu.make_async_copy(lists_v.at[0], row_s.at[1], local.at[5]),
                pltpu.make_async_copy(lists_v.at[1], col_s.at[1], local.at[6]),
                pltpu.make_async_copy(cnt_v, cnt_s.at[1], local.at[7]),
            ]
            for copy in to_smem:
                copy.start()
            for copy in here_copies[:3] + to_smem:
                copy.wait()

        @pl.loop(0, SLOTS)
        def _(s):
            mine = row_s[u, 0, 0, s]
            found = jnp.int32(SLOTS)
            for e in range(SLOTS - 1):
                same = jnp.logical_and(row_s[u, 0, 0, e] == mine, e < s)
                found = jnp.where(same, jnp.int32(e), found)
            prev[u, s] = found

        @pl.loop(0, ROW_BLOCKS)
        def _(t):
            found = jnp.int32(SLOTS)
            for e in range(SLOTS):
                same = jnp.logical_and(row_s[u, 0, 0, e] == t, e < cnt_s[u, 0, 0])
                found = jnp.where(same, jnp.int32(e), found)
            last[u, t] = found

        run[u, SLOTS] = jnp.zeros((2 * BLK, BLK), F32)

    def choose(p):
        wait([scatter[p]])
        sel[p][...] = land[p][owner[1 - c] // 2]
        passed = net.start(sel[p], cand[p].at[1], other)
        cand[p][0] = land[p][owner[c] // 2]
        wait([passed])
        panel[(0,) + piece(p, chip)] = cand[p][(owner[c] + c) % 2]

    ring, plane = {}, {}

    def to_plane(p):
        choose(p)
        mine = panel.at[(0,) + piece(p, chip)]
        plane[p] = net.group()
        for dx, dy in PLANE:
            net.start(mine, mine, device((x + dx) % NX, (y + dy) % NY, c, z), plane[p])

    def step(p, k):
        for e in range(2):
            for sign in (1, -1):
                if k > (4 if (sign == 1) == (e == 0) else 3):
                    continue
                if k > 1:
                    wait([ring[p, k - 1, e, sign]])
                n = BLOCKS[p] // 2
                blocks = pl.ds(FIRST[p] + e * n, n)
                ring[p, k, e, sign] = net.start(
                    panel.at[-sign * (k - 1) % NZ, blocks], panel.at[-sign * k % NZ, blocks],
                    device(x, y, c, (z + sign + NZ) % NZ), None, 2)

    column, chunks, first, second, tail = {}, {}, {}, {}, net.group()
    uv = [(x, y), (y, x)]

    def to_column(p):
        choose(p)
        column[p] = net.group()
        for dz in (1, 7, 2, 6, 3, 5, 4):
            net.start(panel.at[(0,) + piece(p, chip)], panel.at[(NZ - dz,) + piece(p, chip)],
                      device(x, y, c, (z + dz) % NZ), column[p])

    def block(p, h, u, v, skip, n):
        u, v = u % 4, v % 4
        return panel.at[(pl.ds(h * 4 + skip, n),) + piece(p, u * 4 + v if h == 0 else v * 4 + u)]

    def push(h, src, u, v, group=None):
        u, v = u % 4, v % 4
        return net.start(src, src, device(u, v, c, z) if h == 0 else device(v, u, c, z), group, 3)

    def begin(p):
        wait([column[p]])
        for h, (u, v) in enumerate(uv):
            src = block(p, h, u, v, 0, 4)
            first[p, h] = [push(h, src, u + 1, v), push(h, src, u + 3, v)]

    def spread(p, q, du):
        for h, (u, v) in enumerate(uv):
            src = block(p, h, u + du, v, 0, 4)
            chunks[p, q, h] = [push(h, src, u, v + 1), push(h, src, u, v + 3)]

    def pass_on(p):
        for h, (u, v) in enumerate(uv):
            up, down = first[p, h]
            second[p, h] = net.group()
            wait([up])
            push(h, block(p, h, u + 3, v, 0, 2), u + 1, v, second[p, h])
            wait([down])
            push(h, block(p, h, u + 1, v, 2, 2), u + 3, v, second[p, h])

    def relay(p, q, du):
        for h, (u, v) in enumerate(uv):
            up, down = chunks[p, q, h]
            wait([up])
            push(h, block(p, h, u + du, v + 3, 0, 2), u, v + 1, tail)
            wait([down])
            push(h, block(p, h, u + du, v + 1, 2, 2), u, v + 3, tail)

    def last_chunk(p):
        wait([second[p, h] for h in range(2)])
        spread(p, 3, 2)

    net.phase = 1
    to_plane(0)
    to_plane(1)
    to_column(2)
    to_column(3)
    wait([plane[0]])
    step(0, 1)
    wait([plane[1]])
    step(1, 1)
    begin(2)
    spread(2, 0, 0)
    tri_copy = net.start(tri, other_t, other, None, 2)
    begin(3)
    spread(3, 0, 0)
    step(0, 2)
    pass_on(2)
    spread(2, 1, 3)
    spread(2, 2, 1)
    relay(2, 0, 0)
    step(1, 2)
    pass_on(3)
    spread(3, 1, 3)
    spread(3, 2, 1)
    relay(3, 0, 0)
    step(0, 3)
    look_up(0)
    last_chunk(2)
    relay(2, 1, 3)
    relay(2, 2, 1)
    step(1, 3)
    last_chunk(3)
    relay(3, 1, 3)
    relay(3, 2, 1)
    relay(2, 3, 2)
    step(0, 4)
    relay(3, 3, 2)
    step(1, 4)
    look_up(1)
    net.phase = 5
    own_rows = [net.start(panel.at[0, pl.ds(0, FIRST[2])], other_rows.at[pl.ds(0, FIRST[2])], other)]
    wait([tail])
    rest = ROW_BLOCKS - FIRST[2]
    own_rows.append(net.start(panel.at[0, pl.ds(FIRST[2], rest)], other_rows.at[pl.ds(FIRST[2], rest)], other))
    for p in range(2):
        wait([ring[p, 3, 0, -1], ring[p, 3, 1, 1], ring[p, 4, 0, 1], ring[p, 4, 1, -1]])

    here_copies[3].wait()
    wait([tri_copy])
    for u, integrals in enumerate((own_t, other_t)):
        @pl.loop(0, SLOTS, step=2)
        def _(s0, u=u, integrals=integrals):
            products = []
            for i in range(2):
                b = col_s[u, 0, 0, s0 + i]
                rows = panel[(b // ROW_BLOCKS + NZ - z) % NZ, b % ROW_BLOCKS]
                t = integrals[:, s0 + i].reshape(2 * BLK, BLK)
                products.append(jnp.dot(t, rows, preferred_element_type=F32))
            for i in range(2):
                run[u, s0 + i] = products[i] + run[u, prev[u, s0 + i]]
    for u in range(2):
        @pl.loop(0, ROW_BLOCKS)
        def _(t, u=u):
            total = run[u, last[u, t]].astype(BF16)
            at = pl.ds(pl.multiple_of(t * BLK, BLK), BLK)
            for p in range(2):
                half[at, pl.ds((2 * u + p) * BLK, BLK)] = total[p * BLK:(p + 1) * BLK]

    for q in range(2):
        if q == 1:
            wait(own_rows)
        rows = (panel[0] if q == 0 else other_rows[...]).reshape(ROWS, BLK)
        part = lax.dot_general(rows, half[...], (((0,), (0,)), ((), ())), preferred_element_type=F32)
        part = part.reshape(CHIPS // 2, 2, 8, INNER)
        for g in range(2):
            ip[g, q * 4:(q + 1) * 4] = part[:, g].reshape(4, 16, INNER).astype(BF16)

    group = [1 - c, c]
    shares, whole = [net.group() for _ in range(2)], [net.group() for _ in range(2)]
    for k in range(2):
        for dz in range(1, NZ):
            to = (z + dz) % NZ
            net.start(ip.at[group[k], to], ip_land.at[k, dz - 1], device(x, y, c, to), shares[k], 4)
    for k in range(2):
        wait([shares[k]])
        total = ip[group[k], z].astype(F32)
        for dz in range(1, NZ):
            total += ip_land[k, dz - 1].astype(F32)
        ifull[k, z] = total.astype(BF16)
        mine = ifull.at[k, z]
        for dz in range(1, NZ):
            net.start(mine, mine, device(x, y, c, (z + dz) % NZ), whole[k], 4)

    per = TILES // PARTS

    def tile(it, t):
        e = lax.dot_general(it, half[t * TILE:(t + 1) * TILE, :], (((1,), (1,)), ((), ())),
                            preferred_element_type=F32)
        e = e.reshape(CHIPS, 8, TILE)
        return jnp.concatenate([e[..., :BLK], e[..., BLK:]], axis=1)

    wait([whole[0]])
    it = ifull[0].reshape(BLK, INNER)
    swaps = []
    for k in range(PARTS):
        for t in range(per):
            eoth[k, :, :, t * BLK:(t + 1) * BLK] = tile(it, k * per + t).astype(BF16)
        swaps.append(net.start(eoth.at[k], eland.at[k], other))
    wait([whole[1]])
    it = ifull[1].reshape(BLK, INNER)
    shares = []
    for k in range(PARTS):
        for t in range(per):
            eown[k, :, :, t * BLK:(t + 1) * BLK] = tile(it, k * per + t)
        wait([swaps[k]])
        for d in range(CHIPS):
            summed = eown[k, d] + eland[k, (d + 8) % CHIPS].astype(F32)
            eown[k, d] = summed
            ssend[k, d] = summed.astype(BF16)
        shares.append(net.group())
        for i, (dx, dy) in enumerate(PLANE):
            tx, ty = (x + dx) % NX, (y + dy) % NY
            net.start(ssend.at[k, (tx * 4 + ty + 8 * c) % CHIPS], sland.at[k, i], device(tx, ty, c, z), shares[k], 6)
    net.drain()
    for k in range(PARTS):
        wait([shares[k]])
        total = eown[k, (chip + 8 * c) % CHIPS]
        for i in range(CHIPS - 1):
            total += sland[k, i].astype(F32)
        for t in range(per):
            at = (k * per + t) * TILE
            out[:, at:at + BLK] = total[0:8, t * BLK:(t + 1) * BLK]
            out[:, at + BLK:at + TILE] = total[8:16, t * BLK:(t + 1) * BLK]


def body(three_index, home_panels, panel_owner, block_row, block_column, block_count):
    anywhere = pl.BlockSpec(memory_space=pl.ANY)
    smem = pl.BlockSpec(memory_space=pltpu.SMEM)
    dma = pltpu.SemaphoreType.DMA
    vm = pltpu.VMEM
    pieces = [(n // 2, 16, BLK) for n in BLOCKS]
    packed = (PARTS, CHIPS, 16, ROWS // 2 // PARTS)
    out = pl.pallas_call(
        kernel,
        name="exchange",
        out_shape=jax.ShapeDtypeStruct((8, ROWS), F32),
        in_specs=[smem] + [anywhere] * 5,
        out_specs=pl.BlockSpec(memory_space=vm),
        scratch_shapes=[
            vm((NZ, ROW_BLOCKS, BLK, BLK), BF16),
            vm((ROW_BLOCKS, BLK, BLK), BF16),
        ] + [
            vm((CHIPS,) + piece, BF16) for piece in pieces
        ] + [
            vm(piece, BF16) for piece in pieces
        ] + [
            vm((2,) + piece, BF16) for piece in pieces
        ] + [
            vm(three_index.shape, BF16),
            vm(three_index.shape, BF16),
            vm((2,) + block_row.shape, jnp.int32),
            vm(block_count.shape, jnp.int32),
            pltpu.SMEM((2,) + block_row.shape, jnp.int32),
            pltpu.SMEM((2,) + block_row.shape, jnp.int32),
            pltpu.SMEM((2,) + block_count.shape, jnp.int32),
            pltpu.SMEM((2, SLOTS), jnp.int32),
            pltpu.SMEM((2, ROW_BLOCKS), jnp.int32),
            vm((2, SLOTS + 1, 2 * BLK, BLK), F32),
            vm((ROWS, INNER), BF16),
            vm((ROW_BLOCKS, BLK, BLK), BF16),
            vm((2, NZ, 16, INNER), BF16),
            vm((2, NZ - 1, 16, INNER), BF16),
            vm((2, NZ, 16, INNER), BF16),
            vm(packed, F32),
            vm(packed, BF16),
            vm(packed, BF16),
            vm(packed, BF16),
            vm((PARTS, CHIPS - 1) + packed[2:], BF16),
            dma((PHASES + 3,)),
            dma((GROUPS,)),
            dma((8,)),
        ],
        compiler_params=pltpu.CompilerParams(collective_id=0, has_side_effects=True, vmem_limit_bytes=60 * 2**20),
    )(panel_owner, home_panels.reshape(ROW_BLOCKS, BLK, BLK), three_index, block_row, block_column, block_count)
    return out.T


def solution(mesh):
    placed = (
        P("aux", "orb", None, None),
        P("aux", "orb", None),
        P(),
        P("aux", "orb", None),
        P("aux", "orb", None),
        P("aux", "orb"),
    )
    return jax.shard_map(
        body, mesh=mesh, in_specs=placed, out_specs=P("orb", "aux"), check_vma=False
    )
```

```python
import math

import jax
import jax.numpy as jnp
from jax import lax
from jax.experimental import pallas as pl
from jax.experimental.pallas import tpu as pltpu
from jax.sharding import PartitionSpec as P

MESH = pl.DeviceIdType.MESH
BF16 = jnp.bfloat16
F32 = jnp.float32
BLK = 128
NX, NY, NZ = 4, 4, 8
CHIPS = NX * NY
PLANE = [(dx, dy) for dx in range(NX) for dy in range(NY) if (dx, dy) != (0, 0)]
ROWS = 2560
SLOTS = 24
ROW_BLOCKS = ROWS // BLK
BLOCKS = [4, 4, 6, 6]
FIRST = [sum(BLOCKS[:p]) for p in range(4)]
INNER = 512
TILE = 256
TILES = ROWS // TILE
PARTS = 2
UNIT = 16 * BLK
GROUPS = 99
PHASES = 7


def here():
    a = lax.axis_index("aux")
    return a // 8, (a // 2) % 4, a % 2, lax.axis_index("orb")


def device(x, y, core, z):
    return ((x * 4 + y) * 2 + core, z)


class Copies:
    def __init__(self, send, recv, ruler):
        self.send, self.recv, self.ruler = send, recv, ruler
        self.used, self.phase, self.out, self.due = 0, 0, {}, {}

    def group(self):
        self.used += 1
        return self.used - 1

    def start(self, src, dst, target, group=None, phase=None, counted=True):
        group = self.group() if group is None else group
        phase = self.phase if phase is None else phase
        copy = pltpu.make_async_remote_copy(
            src_ref=src, dst_ref=dst, send_sem=self.send.at[phase], recv_sem=self.recv.at[group],
            device_id=target, device_id_type=MESH,
        )
        copy.start()
        size = math.prod(src.shape) // UNIT if counted else 0
        self.out[phase] = self.out.get(phase, 0) + size
        self.due[group] = self.due.get(group, 0) + size
        return group

    def take(self, sem, size):
        fits = [(a, r) for a in range(1, NZ + 1) for r in range(1, 9)
                if size % (a * r) == 0 and size // (a * r) <= ROW_BLOCKS]
        a, r = fits[0]
        ref = self.ruler.at[pl.ds(0, a), pl.ds(0, size // (a * r)), pl.ds(0, r * 16)]
        pltpu.make_async_copy(ref, ref, sem).wait()

    def wait(self, groups):
        for group in groups:
            self.take(self.recv.at[group], self.due.pop(group))

    def drain(self):
        for phase, size in self.out.items():
            self.take(self.send.at[phase], size)
        self.out = {}


def peers(x, y, c, z):
    return (
        [device((x + dx) % NX, (y + dy) % NY, c, z) for dx, dy in PLANE]
        + [device(x, y, c, (z + dz) % NZ) for dz in range(1, NZ)]
        + [device(x, y, 1 - c, z)]
    )


def kernel(owner_h, home, tri, row, col, cnt, out,
           panel, owner, home_v, land0, land1, land2, land3, sel0, sel1, sel2, sel3, cand0, cand1, cand2, cand3, own_t, other_t, lists_v, cnt_v, row_s, col_s, cnt_s, prev, last, run, half,
           other_rows, ip, ip_land, ifull, eown, eoth, eland, ssend, sland, send, recv, local):
    land, sel, cand = (land0, land1, land2, land3), (sel0, sel1, sel2, sel3), (cand0, cand1, cand2, cand3)
    x, y, c, z = here()
    chip = x * 4 + y
    other = device(x, y, 1 - c, z)
    targets = peers(x, y, c, z)
    barrier = pltpu.get_barrier_semaphore()
    for target in targets:
        pl.semaphore_signal(barrier, inc=1, device_id=target, device_id_type=MESH)
    net = Copies(send, recv, panel)
    wait = net.wait

    def piece(p, j):
        n = BLOCKS[p] // 2
        return pl.ds(FIRST[p] + j // 8 * n, n), pl.ds(j % 8 * 16, 16)

    fetch = pltpu.make_async_copy(home, home_v, local.at[0])
    fetch.start()
    here_copies = [
        pltpu.make_async_copy(row, row_s.at[0], local.at[1]),
        pltpu.make_async_copy(col, col_s.at[0], local.at[2]),
        pltpu.make_async_copy(cnt, cnt_s.at[0], local.at[3]),
        pltpu.make_async_copy(tri, own_t, local.at[4]),
    ]
    own_list = pltpu.make_async_copy(owner_h, owner, local.at[8])
    own_list.start()
    for copy in here_copies[:3]:
        copy.start()
    own_list.wait()
    def look_up(u):
        if u == 0:
            for copy in here_copies[:3]:
                copy.wait()
        else:
            for copy in lists:
                copy.wait()
            to_smem = [
                pltpu.make_async_copy(lists_v.at[0], row_s.at[1], local.at[5]),
                pltpu.make_async_copy(lists_v.at[1], col_s.at[1], local.at[6]),
                pltpu.make_async_copy(cnt_v, cnt_s.at[1], local.at[7]),
            ]
            for copy in to_smem:
                copy.start()
            for copy in to_smem:
                copy.wait()

        @pl.loop(0, SLOTS)
        def _(s):
            mine = row_s[u, 0, 0, s]
            found = jnp.int32(SLOTS)
            for e in range(SLOTS - 1):
                same = jnp.logical_and(row_s[u, 0, 0, e] == mine, e < s)
                found = jnp.where(same, jnp.int32(e), found)
            prev[u, s] = found

        @pl.loop(0, ROW_BLOCKS)
        def _(t):
            found = jnp.int32(SLOTS)
            for e in range(SLOTS):
                same = jnp.logical_and(row_s[u, 0, 0, e] == t, e < cnt_s[u, 0, 0])
                found = jnp.where(same, jnp.int32(e), found)
            last[u, t] = found

        run[u, SLOTS] = jnp.zeros((2 * BLK, BLK), F32)

    fetch.wait()
    for p in range(4):
        land[p][chip] = home_v[piece(p, chip)]
    look_up(0)
    pl.semaphore_wait(barrier, len(targets))

    scatter = [net.group() for _ in range(4)]

    def deal(p):
        for dx, dy in PLANE:
            tx, ty = (x + dx) % NX, (y + dy) % NY
            net.start(home_v.at[piece(p, tx * 4 + ty)], land[p].at[chip], device(tx, ty, c, z), scatter[p])

    for p in range(4):
        deal(p)
    lists = [
        pltpu.make_async_remote_copy(
            src_ref=src, dst_ref=dst, send_sem=send.at[PHASES + i], recv_sem=recv.at[net.group()],
            device_id=other, device_id_type=MESH,
        )
        for i, (src, dst) in enumerate(((row, lists_v.at[0]), (col, lists_v.at[1]), (cnt, cnt_v)))
    ]
    for copy in lists:
        copy.start()
    here_copies[3].start()

    look_up(1)

    def choose(p):
        wait([scatter[p]])
        sel[p][...] = land[p][owner[1 - c] // 2]
        passed = net.start(sel[p], cand[p].at[1], other)
        cand[p][0] = land[p][owner[c] // 2]
        wait([passed])
        panel[(0,) + piece(p, chip)] = cand[p][(owner[c] + c) % 2]

    ring, plane = {}, {}

    def to_plane(p):
        choose(p)
        mine = panel.at[(0,) + piece(p, chip)]
        plane[p] = net.group()
        for dx, dy in PLANE:
            net.start(mine, mine, device((x + dx) % NX, (y + dy) % NY, c, z), plane[p])

    def step(p, k):
        for e in range(2):
            for sign in (1, -1):
                if k > (4 if (sign == 1) == (e == 0) else 3):
                    continue
                if k > 1:
                    wait([ring[p, k - 1, e, sign]])
                n = BLOCKS[p] // 2
                blocks = pl.ds(FIRST[p] + e * n, n)
                ring[p, k, e, sign] = net.start(
                    panel.at[-sign * (k - 1) % NZ, blocks], panel.at[-sign * k % NZ, blocks],
                    device(x, y, c, (z + sign + NZ) % NZ), None, 2)

    column, chunks, first, second, tail = {}, {}, {}, {}, net.group()
    uv = [(x, y), (y, x)]

    def to_column(p):
        choose(p)
        column[p] = net.group()
        for dz in (1, 7, 2, 6, 3, 5, 4):
            net.start(panel.at[(0,) + piece(p, chip)], panel.at[(NZ - dz,) + piece(p, chip)],
                      device(x, y, c, (z + dz) % NZ), column[p])

    def block(p, h, u, v, skip, n):
        u, v = u % 4, v % 4
        return panel.at[(pl.ds(h * 4 + skip, n),) + piece(p, u * 4 + v if h == 0 else v * 4 + u)]

    def push(h, src, u, v, group=None):
        u, v = u % 4, v % 4
        return net.start(src, src, device(u, v, c, z) if h == 0 else device(v, u, c, z), group, 3)

    def begin(p):
        wait([column[p]])
        for h, (u, v) in enumerate(uv):
            src = block(p, h, u, v, 0, 4)
            first[p, h] = [push(h, src, u + 1, v), push(h, src, u + 3, v)]

    def spread(p, q, du):
        for h, (u, v) in enumerate(uv):
            src = block(p, h, u + du, v, 0, 4)
            chunks[p, q, h] = [push(h, src, u, v + 1), push(h, src, u, v + 3)]

    def pass_on(p):
        for h, (u, v) in enumerate(uv):
            up, down = first[p, h]
            second[p, h] = net.group()
            wait([up])
            push(h, block(p, h, u + 3, v, 0, 2), u + 1, v, second[p, h])
            wait([down])
            push(h, block(p, h, u + 1, v, 2, 2), u + 3, v, second[p, h])

    def relay(p, q, du):
        for h, (u, v) in enumerate(uv):
            up, down = chunks[p, q, h]
            wait([up])
            push(h, block(p, h, u + du, v + 3, 0, 2), u, v + 1, tail)
            wait([down])
            push(h, block(p, h, u + du, v + 1, 2, 2), u, v + 3, tail)

    def last_chunk(p):
        wait([second[p, h] for h in range(2)])
        spread(p, 3, 2)

    net.phase = 1
    to_plane(0)
    to_plane(1)
    to_column(2)
    to_column(3)
    wait([plane[0]])
    step(0, 1)
    wait([plane[1]])
    step(1, 1)
    begin(2)
    spread(2, 0, 0)
    tri_copy = net.start(tri, other_t, other, None, 2)
    begin(3)
    spread(3, 0, 0)
    step(0, 2)
    pass_on(2)
    spread(2, 1, 3)
    spread(2, 2, 1)
    relay(2, 0, 0)
    step(1, 2)
    pass_on(3)
    spread(3, 1, 3)
    spread(3, 2, 1)
    relay(3, 0, 0)
    step(0, 3)
    last_chunk(2)
    relay(2, 1, 3)
    relay(2, 2, 1)
    step(1, 3)
    last_chunk(3)
    relay(3, 1, 3)
    relay(3, 2, 1)
    relay(2, 3, 2)
    step(0, 4)
    relay(3, 3, 2)
    step(1, 4)
    net.phase = 5
    own_rows = [net.start(panel.at[0, pl.ds(0, FIRST[2])], other_rows.at[pl.ds(0, FIRST[2])], other)]
    wait([tail])
    rest = ROW_BLOCKS - FIRST[2]
    own_rows.append(net.start(panel.at[0, pl.ds(FIRST[2], rest)], other_rows.at[pl.ds(FIRST[2], rest)], other))
    for p in range(2):
        wait([ring[p, 3, 0, -1], ring[p, 3, 1, 1], ring[p, 4, 0, 1], ring[p, 4, 1, -1]])

    here_copies[3].wait()
    wait([tri_copy])
    for u, integrals in enumerate((own_t, other_t)):
        @pl.loop(0, SLOTS, step=8)
        def _(s0, u=u, integrals=integrals):
            products = []
            for i in range(8):
                b = col_s[u, 0, 0, s0 + i]
                rows = panel[(b // ROW_BLOCKS + NZ - z) % NZ, b % ROW_BLOCKS]
                t = integrals[:, s0 + i].reshape(2 * BLK, BLK)
                products.append(jnp.dot(t, rows, preferred_element_type=F32))
            for i in range(8):
                run[u, s0 + i] = products[i] + run[u, prev[u, s0 + i]]
    for u in range(2):
        @pl.loop(0, ROW_BLOCKS, step=4)
        def _(t, u=u):
            for i in range(4):
                total = run[u, last[u, t + i]].astype(BF16)
                at = pl.ds(pl.multiple_of((t + i) * BLK, BLK), BLK)
                for p in range(2):
                    half[at, pl.ds((2 * u + p) * BLK, BLK)] = total[p * BLK:(p + 1) * BLK]

    for q in range(2):
        if q == 1:
            wait(own_rows)
        rows = (panel[0] if q == 0 else other_rows[...]).reshape(ROWS, BLK)
        part = lax.dot_general(rows, half[...], (((0,), (0,)), ((), ())), preferred_element_type=F32)
        part = part.reshape(CHIPS // 2, 2, 8, INNER)
        for g in range(2):
            ip[g, q * 4:(q + 1) * 4] = part[:, g].reshape(4, 16, INNER).astype(BF16)

    shares, whole = [net.group() for _ in range(2)], [net.group() for _ in range(2)]
    for k in range(2):
        for dz in range(1, NZ):
            to = (z + dz) % NZ
            net.start(ip.at[k, to], ip_land.at[k, dz - 1], device(x, y, c, to), shares[k], 4)
    for k in range(2):
        wait([shares[k]])
        total = ip[k, z].astype(F32)
        for dz in range(1, NZ):
            total += ip_land[k, dz - 1].astype(F32)
        ifull[k, z] = total.astype(BF16)
        mine = ifull.at[k, z]
        for dz in range(1, NZ):
            net.start(mine, mine, device(x, y, c, (z + dz) % NZ), whole[k], 4)

    per = TILES // PARTS

    def tile(it, t):
        e = lax.dot_general(it, half[t * TILE:(t + 1) * TILE, :], (((1,), (1,)), ((), ())),
                            preferred_element_type=F32)
        e = e.reshape(CHIPS, 8, TILE)
        return jnp.concatenate([e[..., :BLK], e[..., BLK:]], axis=1)

    swaps = [net.group() for _ in range(PARTS)]
    shares = [net.group() for _ in range(PARTS)]
    for k in range(2):
        wait([whole[k]])
        it = ifull[k].reshape(BLK, INNER)

        @pl.when(c != k)
        def _(k=k, it=it):
            for part in range(PARTS):
                for t in range(per):
                    eoth[part, :, :, t * BLK:(t + 1) * BLK] = tile(it, part * per + t).astype(BF16)
                net.start(eoth.at[part], eland.at[part], other, swaps[part], counted=k == 0)

        @pl.when(c == k)
        def _(k=k, it=it):
            for part in range(PARTS):
                for t in range(per):
                    eown[part, :, :, t * BLK:(t + 1) * BLK] = tile(it, part * per + t)
            for part in range(PARTS):
                net.take(recv.at[swaps[part]], math.prod(eoth.shape[1:]) // UNIT)
                for d in range(CHIPS):
                    summed = eown[part, d] + eland[part, (d + 8) % CHIPS].astype(F32)
                    eown[part, d] = summed
                    ssend[part, d] = summed.astype(BF16)
                for i, (dx, dy) in enumerate(PLANE):
                    tx, ty = (x + dx) % NX, (y + dy) % NY
                    net.start(ssend.at[part, (tx * 4 + ty + 8 * c) % CHIPS], sland.at[part, i],
                              device(tx, ty, c, z), shares[part], 6, k == 0)
    net.drain()
    for k in range(PARTS):
        wait([shares[k]])
        total = eown[k, (chip + 8 * c) % CHIPS]
        for i in range(CHIPS - 1):
            total += sland[k, i].astype(F32)
        for t in range(per):
            at = (k * per + t) * TILE
            out[:, at:at + BLK] = total[0:8, t * BLK:(t + 1) * BLK]
            out[:, at + BLK:at + TILE] = total[8:16, t * BLK:(t + 1) * BLK]


def body(three_index, home_panels, panel_owner, block_row, block_column, block_count):
    anywhere = pl.BlockSpec(memory_space=pl.ANY)
    smem = pl.BlockSpec(memory_space=pltpu.SMEM)
    dma = pltpu.SemaphoreType.DMA
    vm = pltpu.VMEM
    pieces = [(n // 2, 16, BLK) for n in BLOCKS]
    packed = (PARTS, CHIPS, 16, ROWS // 2 // PARTS)
    out = pl.pallas_call(
        kernel,
        name="exchange",
        out_shape=jax.ShapeDtypeStruct((8, ROWS), F32),
        in_specs=[anywhere] * 6,
        out_specs=pl.BlockSpec(memory_space=vm),
        scratch_shapes=[
            vm((NZ, ROW_BLOCKS, BLK, BLK), BF16),
            pltpu.SMEM((32,), jnp.int32),
            vm((ROW_BLOCKS, BLK, BLK), BF16),
        ] + [
            vm((CHIPS,) + piece, BF16) for piece in pieces
        ] + [
            vm(piece, BF16) for piece in pieces
        ] + [
            vm((2,) + piece, BF16) for piece in pieces
        ] + [
            vm(three_index.shape, BF16),
            vm(three_index.shape, BF16),
            vm((2,) + block_row.shape, jnp.int32),
            vm(block_count.shape, jnp.int32),
            pltpu.SMEM((2,) + block_row.shape, jnp.int32),
            pltpu.SMEM((2,) + block_row.shape, jnp.int32),
            pltpu.SMEM((2,) + block_count.shape, jnp.int32),
            pltpu.SMEM((2, SLOTS), jnp.int32),
            pltpu.SMEM((2, ROW_BLOCKS), jnp.int32),
            vm((2, SLOTS + 1, 2 * BLK, BLK), F32),
            vm((ROWS, INNER), BF16),
            vm((ROW_BLOCKS, BLK, BLK), BF16),
            vm((2, NZ, 16, INNER), BF16),
            vm((2, NZ - 1, 16, INNER), BF16),
            vm((2, NZ, 16, INNER), BF16),
            vm(packed, F32),
            vm(packed, BF16),
            vm(packed, BF16),
            vm(packed, BF16),
            vm((PARTS, CHIPS - 1) + packed[2:], BF16),
            dma((PHASES + 3,)),
            dma((GROUPS,)),
            dma((9,)),
        ],
        compiler_params=pltpu.CompilerParams(collective_id=0, has_side_effects=True, vmem_limit_bytes=48 * 2**20),
    )(*[
        pltpu.with_memory_space_constraint(value, pltpu.HBM)
        for value in (panel_owner, home_panels.reshape(ROW_BLOCKS, BLK, BLK), three_index, block_row, block_column)
    ], block_count)
    return out.T


def solution(mesh):
    placed = (
        P("aux", "orb", None, None),
        P("aux", "orb", None),
        P(),
        P("aux", "orb", None),
        P("aux", "orb", None),
        P("aux", "orb"),
    )
    return jax.shard_map(
        body, mesh=mesh, in_specs=placed, out_specs=P("orb", "aux"), check_vma=False
    )
```

```python
import math

import jax
import jax.numpy as jnp
from jax import lax
from jax.experimental import pallas as pl
from jax.experimental.pallas import tpu as pltpu
from jax.sharding import PartitionSpec as P

MESH = pl.DeviceIdType.MESH
BF16 = jnp.bfloat16
F32 = jnp.float32
BLK = 128
NX, NY, NZ = 4, 4, 8
CHIPS = NX * NY
PLANE = [(2, 2), (2, 1), (2, 3), (1, 2), (3, 2), (2, 0), (0, 2), (1, 1), (1, 3), (3, 1), (3, 3), (1, 0), (3, 0), (0, 1), (0, 3)]
LINE = (4, 3, 5, 2, 6, 1, 7)
ROWS = 2560
SLOTS = 24
ROW_BLOCKS = ROWS // BLK
BLOCKS = [4, 4, 6, 6]
FIRST = [sum(BLOCKS[:p]) for p in range(4)]
INNER = 512
TILE = 256
TILES = ROWS // TILE
PARTS = 2
UNIT = 16 * BLK
GROUPS = 99
PHASES = 7


def here():
    a = lax.axis_index("aux")
    return a // 8, (a // 2) % 4, a % 2, lax.axis_index("orb")


def device(x, y, core, z):
    return ((x * 4 + y) * 2 + core, z)


class Copies:
    def __init__(self, send, recv, ruler):
        self.send, self.recv, self.ruler = send, recv, ruler
        self.used, self.phase, self.out, self.due = 0, 0, {}, {}

    def group(self):
        self.used += 1
        return self.used - 1

    def start(self, src, dst, target, group=None, phase=None, counted=True):
        group = self.group() if group is None else group
        phase = self.phase if phase is None else phase
        copy = pltpu.make_async_remote_copy(
            src_ref=src, dst_ref=dst, send_sem=self.send.at[phase], recv_sem=self.recv.at[group],
            device_id=target, device_id_type=MESH,
        )
        copy.start()
        size = math.prod(src.shape) // UNIT if counted else 0
        self.out[phase] = self.out.get(phase, 0) + size
        self.due[group] = self.due.get(group, 0) + size
        return group

    def take(self, sem, size):
        fits = [(a, r) for a in range(1, NZ + 1) for r in range(1, 9)
                if size % (a * r) == 0 and size // (a * r) <= ROW_BLOCKS]
        a, r = fits[0]
        ref = self.ruler.at[pl.ds(0, a), pl.ds(0, size // (a * r)), pl.ds(0, r * 16)]
        pltpu.make_async_copy(ref, ref, sem).wait()

    def wait(self, groups):
        for group in groups:
            self.take(self.recv.at[group], self.due.pop(group))

    def drain(self):
        for phase, size in self.out.items():
            self.take(self.send.at[phase], size)
        self.out = {}


def peers(x, y, c, z):
    return (
        [device((x + dx) % NX, (y + dy) % NY, c, z) for dx, dy in PLANE]
        + [device(x, y, c, (z + dz) % NZ) for dz in LINE]
        + [device(x, y, 1 - c, z)]
    )


def kernel(owner_h, home, tri, row, col, cnt, out,
           panel, owner, home_v, land0, land1, land2, land3, sel0, sel1, sel2, sel3, cand0, cand1, cand2, cand3, own_t, other_t, lists_v, cnt_v, row_s, col_s, cnt_s, prev, last, run, half,
           other_rows, ip, ip_land, ifull, eown, eoth, eland, ssend, sland, send, recv, local):
    land, sel, cand = (land0, land1, land2, land3), (sel0, sel1, sel2, sel3), (cand0, cand1, cand2, cand3)
    x, y, c, z = here()
    chip = x * 4 + y
    other = device(x, y, 1 - c, z)
    targets = peers(x, y, c, z)
    barrier = pltpu.get_barrier_semaphore()
    for target in targets:
        pl.semaphore_signal(barrier, inc=1, device_id=target, device_id_type=MESH)
    net = Copies(send, recv, panel)
    wait = net.wait

    def piece(p, j):
        n = BLOCKS[p] // 2
        return pl.ds(FIRST[p] + j // 8 * n, n), pl.ds(j % 8 * 16, 16)

    fetch = pltpu.make_async_copy(home, home_v, local.at[0])
    fetch.start()
    here_copies = [
        pltpu.make_async_copy(row, row_s.at[0], local.at[1]),
        pltpu.make_async_copy(col, col_s.at[0], local.at[2]),
        pltpu.make_async_copy(cnt, cnt_s.at[0], local.at[3]),
        pltpu.make_async_copy(tri, own_t, local.at[4]),
    ]
    own_list = pltpu.make_async_copy(owner_h, owner, local.at[8])
    own_list.start()
    for copy in here_copies[:3]:
        copy.start()
    own_list.wait()
    def look_up(u):
        if u == 0:
            for copy in here_copies[:3]:
                copy.wait()
        else:
            for copy in lists:
                copy.wait()
            to_smem = [
                pltpu.make_async_copy(lists_v.at[0], row_s.at[1], local.at[5]),
                pltpu.make_async_copy(lists_v.at[1], col_s.at[1], local.at[6]),
                pltpu.make_async_copy(cnt_v, cnt_s.at[1], local.at[7]),
            ]
            for copy in to_smem:
                copy.start()
            for copy in to_smem:
                copy.wait()

        @pl.loop(0, SLOTS)
        def _(s):
            mine = row_s[u, 0, 0, s]
            found = jnp.int32(SLOTS)
            for e in range(SLOTS - 1):
                same = jnp.logical_and(row_s[u, 0, 0, e] == mine, e < s)
                found = jnp.where(same, jnp.int32(e), found)
            prev[u, s] = found

        @pl.loop(0, ROW_BLOCKS)
        def _(t):
            found = jnp.int32(SLOTS)
            for e in range(SLOTS):
                same = jnp.logical_and(row_s[u, 0, 0, e] == t, e < cnt_s[u, 0, 0])
                found = jnp.where(same, jnp.int32(e), found)
            last[u, t] = found

        run[u, SLOTS] = jnp.zeros((2 * BLK, BLK), F32)

    fetch.wait()
    for p in range(4):
        land[p][chip] = home_v[piece(p, chip)]
    look_up(0)
    pl.semaphore_wait(barrier, len(targets))

    scatter = [net.group() for _ in range(4)]

    def deal(p):
        for dx, dy in PLANE:
            tx, ty = (x + dx) % NX, (y + dy) % NY
            net.start(home_v.at[piece(p, tx * 4 + ty)], land[p].at[chip], device(tx, ty, c, z), scatter[p])

    for p in range(4):
        deal(p)
    lists = [
        pltpu.make_async_remote_copy(
            src_ref=src, dst_ref=dst, send_sem=send.at[PHASES + i], recv_sem=recv.at[net.group()],
            device_id=other, device_id_type=MESH,
        )
        for i, (src, dst) in enumerate(((row, lists_v.at[0]), (col, lists_v.at[1]), (cnt, cnt_v)))
    ]
    for copy in lists:
        copy.start()
    here_copies[3].start()

    look_up(1)

    def choose(p):
        wait([scatter[p]])
        sel[p][...] = land[p][owner[1 - c] // 2]
        passed = net.start(sel[p], cand[p].at[1], other)
        cand[p][0] = land[p][owner[c] // 2]
        wait([passed])
        panel[(0,) + piece(p, chip)] = cand[p][(owner[c] + c) % 2]

    ring, plane = {}, {}

    def to_plane(p):
        choose(p)
        mine = panel.at[(0,) + piece(p, chip)]
        plane[p] = net.group()
        for dx, dy in PLANE:
            net.start(mine, mine, device((x + dx) % NX, (y + dy) % NY, c, z), plane[p])

    def step(p, k):
        for e in range(2):
            for sign in (1, -1):
                if k > (4 if (sign == 1) == (e == 0) else 3):
                    continue
                if k > 1:
                    wait([ring[p, k - 1, e, sign]])
                n = BLOCKS[p] // 2
                blocks = pl.ds(FIRST[p] + e * n, n)
                ring[p, k, e, sign] = net.start(
                    panel.at[-sign * (k - 1) % NZ, blocks], panel.at[-sign * k % NZ, blocks],
                    device(x, y, c, (z + sign + NZ) % NZ), None, 2)

    column, chunks, first, second, tail = {}, {}, {}, {}, net.group()
    uv = [(x, y), (y, x)]

    def to_column(p):
        choose(p)
        column[p] = net.group()
        for dz in LINE:
            net.start(panel.at[(0,) + piece(p, chip)], panel.at[(NZ - dz,) + piece(p, chip)],
                      device(x, y, c, (z + dz) % NZ), column[p])

    def block(p, h, u, v, skip, n):
        u, v = u % 4, v % 4
        return panel.at[(pl.ds(h * 4 + skip, n),) + piece(p, u * 4 + v if h == 0 else v * 4 + u)]

    def push(h, src, u, v, group=None):
        u, v = u % 4, v % 4
        return net.start(src, src, device(u, v, c, z) if h == 0 else device(v, u, c, z), group, 3)

    def begin(p):
        wait([column[p]])
        for h, (u, v) in enumerate(uv):
            src = block(p, h, u, v, 0, 4)
            first[p, h] = [push(h, src, u + 1, v), push(h, src, u + 3, v)]

    def spread(p, q, du):
        for h, (u, v) in enumerate(uv):
            src = block(p, h, u + du, v, 0, 4)
            chunks[p, q, h] = [push(h, src, u, v + 1), push(h, src, u, v + 3)]

    def pass_on(p):
        for h, (u, v) in enumerate(uv):
            up, down = first[p, h]
            second[p, h] = net.group()
            wait([up])
            push(h, block(p, h, u + 3, v, 0, 2), u + 1, v, second[p, h])
            wait([down])
            push(h, block(p, h, u + 1, v, 2, 2), u + 3, v, second[p, h])

    def relay(p, q, du):
        for h, (u, v) in enumerate(uv):
            up, down = chunks[p, q, h]
            wait([up])
            push(h, block(p, h, u + du, v + 3, 0, 2), u, v + 1, tail)
            wait([down])
            push(h, block(p, h, u + du, v + 1, 2, 2), u, v + 3, tail)

    def last_chunk(p):
        wait([second[p, h] for h in range(2)])
        spread(p, 3, 2)

    net.phase = 1
    to_plane(0)
    to_plane(1)
    to_column(2)
    to_column(3)
    wait([plane[0]])
    step(0, 1)
    wait([plane[1]])
    step(1, 1)
    begin(2)
    spread(2, 0, 0)
    tri_copy = net.start(tri, other_t, other, None, 2)
    begin(3)
    spread(3, 0, 0)
    step(0, 2)
    pass_on(2)
    spread(2, 1, 3)
    spread(2, 2, 1)
    relay(2, 0, 0)
    step(1, 2)
    pass_on(3)
    spread(3, 1, 3)
    spread(3, 2, 1)
    relay(3, 0, 0)
    step(0, 3)
    last_chunk(2)
    relay(2, 1, 3)
    relay(2, 2, 1)
    step(1, 3)
    last_chunk(3)
    relay(3, 1, 3)
    relay(3, 2, 1)
    relay(2, 3, 2)
    step(0, 4)
    relay(3, 3, 2)
    step(1, 4)
    net.phase = 5
    own_rows = [net.start(panel.at[0, pl.ds(0, FIRST[2])], other_rows.at[pl.ds(0, FIRST[2])], other)]
    wait([tail])
    rest = ROW_BLOCKS - FIRST[2]
    own_rows.append(net.start(panel.at[0, pl.ds(FIRST[2], rest)], other_rows.at[pl.ds(FIRST[2], rest)], other))
    for p in range(2):
        wait([ring[p, 3, 0, -1], ring[p, 3, 1, 1], ring[p, 4, 0, 1], ring[p, 4, 1, -1]])

    here_copies[3].wait()
    wait([tri_copy])
    for u, integrals in enumerate((own_t, other_t)):
        @pl.loop(0, SLOTS, step=8)
        def _(s0, u=u, integrals=integrals):
            products = []
            for i in range(8):
                b = col_s[u, 0, 0, s0 + i]
                rows = panel[(b // ROW_BLOCKS + NZ - z) % NZ, b % ROW_BLOCKS]
                t = integrals[:, s0 + i].reshape(2 * BLK, BLK)
                products.append(jnp.dot(t, rows, preferred_element_type=F32))
            for i in range(8):
                run[u, s0 + i] = products[i] + run[u, prev[u, s0 + i]]
    for u in range(2):
        @pl.loop(0, ROW_BLOCKS, step=4)
        def _(t, u=u):
            for i in range(4):
                total = run[u, last[u, t + i]].astype(BF16)
                at = pl.ds(pl.multiple_of((t + i) * BLK, BLK), BLK)
                for p in range(2):
                    half[at, pl.ds((2 * u + p) * BLK, BLK)] = total[p * BLK:(p + 1) * BLK]

    for q in range(2):
        if q == 1:
            wait(own_rows)
        rows = (panel[0] if q == 0 else other_rows[...]).reshape(ROWS, BLK)
        part = lax.dot_general(rows, half[...], (((0,), (0,)), ((), ())), preferred_element_type=F32)
        part = part.reshape(CHIPS // 2, 2, 8, INNER)
        for g in range(2):
            ip[g, q * 4:(q + 1) * 4] = part[:, g].reshape(4, 16, INNER).astype(BF16)

    shares, whole = [net.group() for _ in range(2)], [net.group() for _ in range(2)]
    for k in range(2):
        for dz in LINE:
            to = (z + dz) % NZ
            net.start(ip.at[k, to], ip_land.at[k, dz - 1], device(x, y, c, to), shares[k], 4)
    for k in range(2):
        wait([shares[k]])
        total = ip[k, z].astype(F32)
        for dz in range(1, NZ):
            total += ip_land[k, dz - 1].astype(F32)
        ifull[k, z] = total.astype(BF16)
        mine = ifull.at[k, z]
        for dz in LINE:
            net.start(mine, mine, device(x, y, c, (z + dz) % NZ), whole[k], 4)

    per = TILES // PARTS

    def tile(it, t):
        e = lax.dot_general(it, half[t * TILE:(t + 1) * TILE, :], (((1,), (1,)), ((), ())),
                            preferred_element_type=F32)
        e = e.reshape(CHIPS, 8, TILE)
        return jnp.concatenate([e[..., :BLK], e[..., BLK:]], axis=1)

    swaps = [net.group() for _ in range(PARTS)]
    shares = [net.group() for _ in range(PARTS)]
    for k in range(2):
        wait([whole[k]])
        it = ifull[k].reshape(BLK, INNER)

        @pl.when(c != k)
        def _(k=k, it=it):
            for part in range(PARTS):
                for t in range(per):
                    eoth[part, :, :, t * BLK:(t + 1) * BLK] = tile(it, part * per + t).astype(BF16)
                net.start(eoth.at[part], eland.at[part], other, swaps[part], counted=k == 0)

        @pl.when(c == k)
        def _(k=k, it=it):
            for part in range(PARTS):
                for t in range(per):
                    eown[part, :, :, t * BLK:(t + 1) * BLK] = tile(it, part * per + t)
            for part in range(PARTS):
                net.take(recv.at[swaps[part]], math.prod(eoth.shape[1:]) // UNIT)
                for d in range(CHIPS):
                    summed = eown[part, d] + eland[part, (d + 8) % CHIPS].astype(F32)
                    eown[part, d] = summed
                    ssend[part, d] = summed.astype(BF16)
                for i, (dx, dy) in enumerate(PLANE):
                    tx, ty = (x + dx) % NX, (y + dy) % NY
                    net.start(ssend.at[part, (tx * 4 + ty + 8 * c) % CHIPS], sland.at[part, i],
                              device(tx, ty, c, z), shares[part], 6, k == 0)
    net.drain()
    for k in range(PARTS):
        wait([shares[k]])
        total = eown[k, (chip + 8 * c) % CHIPS]
        for i in range(CHIPS - 1):
            total += sland[k, i].astype(F32)
        for t in range(per):
            at = (k * per + t) * TILE
            out[:, at:at + BLK] = total[0:8, t * BLK:(t + 1) * BLK]
            out[:, at + BLK:at + TILE] = total[8:16, t * BLK:(t + 1) * BLK]


def body(three_index, home_panels, panel_owner, block_row, block_column, block_count):
    anywhere = pl.BlockSpec(memory_space=pl.ANY)
    smem = pl.BlockSpec(memory_space=pltpu.SMEM)
    dma = pltpu.SemaphoreType.DMA
    vm = pltpu.VMEM
    pieces = [(n // 2, 16, BLK) for n in BLOCKS]
    packed = (PARTS, CHIPS, 16, ROWS // 2 // PARTS)
    out = pl.pallas_call(
        kernel,
        name="exchange",
        out_shape=jax.ShapeDtypeStruct((8, ROWS), F32),
        in_specs=[anywhere] * 6,
        out_specs=pl.BlockSpec(memory_space=vm),
        scratch_shapes=[
            vm((NZ, ROW_BLOCKS, BLK, BLK), BF16),
            pltpu.SMEM((32,), jnp.int32),
            vm((ROW_BLOCKS, BLK, BLK), BF16),
        ] + [
            vm((CHIPS,) + piece, BF16) for piece in pieces
        ] + [
            vm(piece, BF16) for piece in pieces
        ] + [
            vm((2,) + piece, BF16) for piece in pieces
        ] + [
            vm(three_index.shape, BF16),
            vm(three_index.shape, BF16),
            vm((2,) + block_row.shape, jnp.int32),
            vm(block_count.shape, jnp.int32),
            pltpu.SMEM((2,) + block_row.shape, jnp.int32),
            pltpu.SMEM((2,) + block_row.shape, jnp.int32),
            pltpu.SMEM((2,) + block_count.shape, jnp.int32),
            pltpu.SMEM((2, SLOTS), jnp.int32),
            pltpu.SMEM((2, ROW_BLOCKS), jnp.int32),
            vm((2, SLOTS + 1, 2 * BLK, BLK), F32),
            vm((ROWS, INNER), BF16),
            vm((ROW_BLOCKS, BLK, BLK), BF16),
            vm((2, NZ, 16, INNER), BF16),
            vm((2, NZ - 1, 16, INNER), BF16),
            vm((2, NZ, 16, INNER), BF16),
            vm(packed, F32),
            vm(packed, BF16),
            vm(packed, BF16),
            vm(packed, BF16),
            vm((PARTS, CHIPS - 1) + packed[2:], BF16),
            dma((PHASES + 3,)),
            dma((GROUPS,)),
            dma((9,)),
        ],
        compiler_params=pltpu.CompilerParams(collective_id=0, has_side_effects=True, vmem_limit_bytes=48 * 2**20),
    )(*[
        pltpu.with_memory_space_constraint(value, pltpu.HBM)
        for value in (panel_owner, home_panels.reshape(ROW_BLOCKS, BLK, BLK), three_index, block_row, block_column)
    ], block_count)
    return out.T


def solution(mesh):
    placed = (
        P("aux", "orb", None, None),
        P("aux", "orb", None),
        P(),
        P("aux", "orb", None),
        P("aux", "orb", None),
        P("aux", "orb"),
    )
    return jax.shard_map(
        body, mesh=mesh, in_specs=placed, out_specs=P("orb", "aux"), check_vma=False
    )
```

```python
import math

import jax
import jax.numpy as jnp
from jax import lax
from jax.experimental import pallas as pl
from jax.experimental.pallas import tpu as pltpu
from jax.sharding import PartitionSpec as P

MESH = pl.DeviceIdType.MESH
BF16 = jnp.bfloat16
F32 = jnp.float32
BLK = 128
NX, NY, NZ = 4, 4, 8
CHIPS = NX * NY
PLANE = [(2, 2), (2, 1), (2, 3), (1, 2), (3, 2), (2, 0), (0, 2), (1, 1), (1, 3), (3, 1), (3, 3), (1, 0), (3, 0), (0, 1), (0, 3)]
LINE = (4, 3, 5, 2, 6, 1, 7)
ROWS = 2560
SLOTS = 24
ROW_BLOCKS = ROWS // BLK
BLOCKS = [4, 4, 6, 6]
FIRST = [sum(BLOCKS[:p]) for p in range(4)]
INNER = 512
TILE = 256
TILES = ROWS // TILE
PARTS = 2
UNIT = 16 * BLK
GROUPS = 99
PHASES = 7


def here():
    a = lax.axis_index("aux")
    return a // 8, (a // 2) % 4, a % 2, lax.axis_index("orb")


def device(x, y, core, z):
    return ((x * 4 + y) * 2 + core, z)


class Copies:
    def __init__(self, send, recv, ruler):
        self.send, self.recv, self.ruler = send, recv, ruler
        self.used, self.phase, self.out, self.due = 0, 0, {}, {}

    def group(self):
        self.used += 1
        return self.used - 1

    def start(self, src, dst, target, group=None, phase=None, counted=True):
        group = self.group() if group is None else group
        phase = self.phase if phase is None else phase
        copy = pltpu.make_async_remote_copy(
            src_ref=src, dst_ref=dst, send_sem=self.send.at[phase], recv_sem=self.recv.at[group],
            device_id=target, device_id_type=MESH,
        )
        copy.start()
        size = math.prod(src.shape) // UNIT if counted else 0
        self.out[phase] = self.out.get(phase, 0) + size
        self.due[group] = self.due.get(group, 0) + size
        return group

    def take(self, sem, size):
        fits = [(a, r) for a in range(1, NZ + 1) for r in range(1, 9)
                if size % (a * r) == 0 and size // (a * r) <= ROW_BLOCKS]
        a, r = fits[0]
        ref = self.ruler.at[pl.ds(0, a), pl.ds(0, size // (a * r)), pl.ds(0, r * 16)]
        pltpu.make_async_copy(ref, ref, sem).wait()

    def wait(self, groups):
        for group in groups:
            self.take(self.recv.at[group], self.due.pop(group))

    def drain(self):
        for phase, size in self.out.items():
            self.take(self.send.at[phase], size)
        self.out = {}


def peers(x, y, c, z):
    return (
        [device((x + dx) % NX, (y + dy) % NY, c, z) for dx, dy in PLANE]
        + [device(x, y, c, (z + dz) % NZ) for dz in LINE]
        + [device(x, y, 1 - c, z)]
    )


def kernel(owner_h, home, tri, row, col, cnt, out,
           panel, owner, home_v, land0, land1, land2, land3, sel0, sel1, sel2, sel3, cand0, cand1, cand2, cand3, own_t, other_t, lists_v, cnt_v, row_s, col_s, cnt_s, prev, last, run, half,
           other_rows, ip, ip_land, ifull, eown, eoth, eland, ssend, sland, send, recv, local):
    land, sel, cand = (land0, land1, land2, land3), (sel0, sel1, sel2, sel3), (cand0, cand1, cand2, cand3)
    x, y, c, z = here()
    chip = x * 4 + y
    other = device(x, y, 1 - c, z)
    targets = peers(x, y, c, z)
    barrier = pltpu.get_barrier_semaphore()
    for target in targets:
        pl.semaphore_signal(barrier, inc=1, device_id=target, device_id_type=MESH)
    net = Copies(send, recv, panel)
    wait = net.wait

    def piece(p, j):
        n = BLOCKS[p] // 2
        return pl.ds(FIRST[p] + j // 8 * n, n), pl.ds(j % 8 * 16, 16)

    fetch = pltpu.make_async_copy(home, home_v, local.at[0])
    fetch.start()
    here_copies = [
        pltpu.make_async_copy(row, row_s.at[0], local.at[1]),
        pltpu.make_async_copy(col, col_s.at[0], local.at[2]),
        pltpu.make_async_copy(cnt, cnt_s.at[0], local.at[3]),
        pltpu.make_async_copy(tri, own_t, local.at[4]),
    ]
    own_list = pltpu.make_async_copy(owner_h, owner, local.at[8])
    own_list.start()
    for copy in here_copies[:3]:
        copy.start()
    own_list.wait()
    def look_up(u):
        if u == 0:
            for copy in here_copies[:3]:
                copy.wait()
        else:
            for copy in lists:
                copy.wait()
            to_smem = [
                pltpu.make_async_copy(lists_v.at[0], row_s.at[1], local.at[5]),
                pltpu.make_async_copy(lists_v.at[1], col_s.at[1], local.at[6]),
                pltpu.make_async_copy(cnt_v, cnt_s.at[1], local.at[7]),
            ]
            for copy in to_smem:
                copy.start()
            for copy in to_smem:
                copy.wait()

        @pl.loop(0, SLOTS)
        def _(s):
            mine = row_s[u, 0, 0, s]
            found = jnp.int32(SLOTS)
            for e in range(SLOTS - 1):
                same = jnp.logical_and(row_s[u, 0, 0, e] == mine, e < s)
                found = jnp.where(same, jnp.int32(e), found)
            prev[u, s] = found

        @pl.loop(0, ROW_BLOCKS)
        def _(t):
            found = jnp.int32(SLOTS)
            for e in range(SLOTS):
                same = jnp.logical_and(row_s[u, 0, 0, e] == t, e < cnt_s[u, 0, 0])
                found = jnp.where(same, jnp.int32(e), found)
            last[u, t] = found

        run[u, SLOTS] = jnp.zeros((2 * BLK, BLK), F32)

    fetch.wait()
    for p in range(4):
        land[p][chip] = home_v[piece(p, chip)]
    look_up(0)
    pl.semaphore_wait(barrier, len(targets))

    scatter = [net.group() for _ in range(4)]

    def deal(p):
        for dx, dy in PLANE:
            tx, ty = (x + dx) % NX, (y + dy) % NY
            net.start(home_v.at[piece(p, tx * 4 + ty)], land[p].at[chip], device(tx, ty, c, z), scatter[p])

    for p in (2, 0, 3, 1):
        deal(p)
    lists = [
        pltpu.make_async_remote_copy(
            src_ref=src, dst_ref=dst, send_sem=send.at[PHASES + i], recv_sem=recv.at[net.group()],
            device_id=other, device_id_type=MESH,
        )
        for i, (src, dst) in enumerate(((row, lists_v.at[0]), (col, lists_v.at[1]), (cnt, cnt_v)))
    ]
    for copy in lists:
        copy.start()
    here_copies[3].start()

    look_up(1)

    def choose(p):
        wait([scatter[p]])
        sel[p][...] = land[p][owner[1 - c] // 2]
        passed = net.start(sel[p], cand[p].at[1], other)
        cand[p][0] = land[p][owner[c] // 2]
        wait([passed])
        panel[(0,) + piece(p, chip)] = cand[p][(owner[c] + c) % 2]

    ring, plane = {}, {}

    def to_plane(p):
        choose(p)
        mine = panel.at[(0,) + piece(p, chip)]
        plane[p] = net.group()
        for dx, dy in PLANE:
            net.start(mine, mine, device((x + dx) % NX, (y + dy) % NY, c, z), plane[p])

    def step(p, k):
        for e in range(2):
            for sign in (1, -1):
                if k > (4 if (sign == 1) == (e == 0) else 3):
                    continue
                if k > 1:
                    wait([ring[p, k - 1, e, sign]])
                n = BLOCKS[p] // 2
                blocks = pl.ds(FIRST[p] + e * n, n)
                ring[p, k, e, sign] = net.start(
                    panel.at[-sign * (k - 1) % NZ, blocks], panel.at[-sign * k % NZ, blocks],
                    device(x, y, c, (z + sign + NZ) % NZ), None, 2)

    column, chunks, first, second, tail = {}, {}, {}, {}, net.group()
    uv = [(x, y), (y, x)]

    def to_column(p):
        choose(p)
        column[p] = net.group()
        for dz in LINE:
            net.start(panel.at[(0,) + piece(p, chip)], panel.at[(NZ - dz,) + piece(p, chip)],
                      device(x, y, c, (z + dz) % NZ), column[p])

    def block(p, h, u, v, skip, n):
        u, v = u % 4, v % 4
        return panel.at[(pl.ds(h * 4 + skip, n),) + piece(p, u * 4 + v if h == 0 else v * 4 + u)]

    def push(h, src, u, v, group=None):
        u, v = u % 4, v % 4
        return net.start(src, src, device(u, v, c, z) if h == 0 else device(v, u, c, z), group, 3)

    def begin(p):
        wait([column[p]])
        for h, (u, v) in enumerate(uv):
            src = block(p, h, u, v, 0, 4)
            first[p, h] = [push(h, src, u + 1, v), push(h, src, u + 3, v)]

    def spread(p, q, du):
        for h, (u, v) in enumerate(uv):
            src = block(p, h, u + du, v, 0, 4)
            chunks[p, q, h] = [push(h, src, u, v + 1), push(h, src, u, v + 3)]

    def pass_on(p):
        for h, (u, v) in enumerate(uv):
            up, down = first[p, h]
            second[p, h] = net.group()
            wait([up])
            push(h, block(p, h, u + 3, v, 0, 2), u + 1, v, second[p, h])
            wait([down])
            push(h, block(p, h, u + 1, v, 2, 2), u + 3, v, second[p, h])

    def relay(p, q, du):
        for h, (u, v) in enumerate(uv):
            up, down = chunks[p, q, h]
            wait([up])
            push(h, block(p, h, u + du, v + 3, 0, 2), u, v + 1, tail)
            wait([down])
            push(h, block(p, h, u + du, v + 1, 2, 2), u, v + 3, tail)

    def last_chunk(p):
        wait([second[p, h] for h in range(2)])
        spread(p, 3, 2)

    net.phase = 1
    to_column(2)
    to_plane(0)
    to_column(3)
    to_plane(1)
    begin(2)
    spread(2, 0, 0)
    wait([plane[0]])
    step(0, 1)
    begin(3)
    spread(3, 0, 0)
    tri_copy = net.start(tri, other_t, other, None, 2)
    wait([plane[1]])
    step(1, 1)
    pass_on(2)
    spread(2, 1, 3)
    spread(2, 2, 1)
    relay(2, 0, 0)
    step(0, 2)
    pass_on(3)
    spread(3, 1, 3)
    spread(3, 2, 1)
    relay(3, 0, 0)
    step(1, 2)
    last_chunk(2)
    relay(2, 1, 3)
    relay(2, 2, 1)
    step(0, 3)
    last_chunk(3)
    relay(3, 1, 3)
    step(1, 3)
    relay(3, 2, 1)
    relay(2, 3, 2)
    step(0, 4)
    relay(3, 3, 2)
    step(1, 4)
    net.phase = 5
    own_rows = [net.start(panel.at[0, pl.ds(0, FIRST[2])], other_rows.at[pl.ds(0, FIRST[2])], other)]
    wait([tail])
    rest = ROW_BLOCKS - FIRST[2]
    own_rows.append(net.start(panel.at[0, pl.ds(FIRST[2], rest)], other_rows.at[pl.ds(FIRST[2], rest)], other))
    for p in range(2):
        wait([ring[p, 3, 0, -1], ring[p, 3, 1, 1], ring[p, 4, 0, 1], ring[p, 4, 1, -1]])

    here_copies[3].wait()
    wait([tri_copy])
    for u, integrals in enumerate((own_t, other_t)):
        @pl.loop(0, SLOTS, step=8)
        def _(s0, u=u, integrals=integrals):
            products = []
            for i in range(8):
                b = col_s[u, 0, 0, s0 + i]
                rows = panel[(b // ROW_BLOCKS + NZ - z) % NZ, b % ROW_BLOCKS]
                t = integrals[:, s0 + i].reshape(2 * BLK, BLK)
                products.append(jnp.dot(t, rows, preferred_element_type=F32))
            for i in range(8):
                run[u, s0 + i] = products[i] + run[u, prev[u, s0 + i]]
    for u in range(2):
        @pl.loop(0, ROW_BLOCKS, step=4)
        def _(t, u=u):
            for i in range(4):
                total = run[u, last[u, t + i]].astype(BF16)
                at = pl.ds(pl.multiple_of((t + i) * BLK, BLK), BLK)
                for p in range(2):
                    half[at, pl.ds((2 * u + p) * BLK, BLK)] = total[p * BLK:(p + 1) * BLK]

    for q in range(2):
        if q == 1:
            wait(own_rows)
        rows = (panel[0] if q == 0 else other_rows[...]).reshape(ROWS, BLK)
        part = lax.dot_general(rows, half[...], (((0,), (0,)), ((), ())), preferred_element_type=F32)
        part = part.reshape(CHIPS // 2, 2, 8, INNER)
        for g in range(2):
            ip[g, q * 4:(q + 1) * 4] = part[:, g].reshape(4, 16, INNER).astype(BF16)

    shares, whole = [net.group() for _ in range(2)], [net.group() for _ in range(2)]
    for k in range(2):
        for dz in LINE:
            to = (z + dz) % NZ
            net.start(ip.at[k, to], ip_land.at[k, dz - 1], device(x, y, c, to), shares[k], 4)
    for k in range(2):
        wait([shares[k]])
        total = ip[k, z].astype(F32)
        for dz in range(1, NZ):
            total += ip_land[k, dz - 1].astype(F32)
        ifull[k, z] = total.astype(BF16)
        mine = ifull.at[k, z]
        for dz in LINE:
            net.start(mine, mine, device(x, y, c, (z + dz) % NZ), whole[k], 4)

    per = TILES // PARTS

    def tile(it, t):
        e = lax.dot_general(it, half[t * TILE:(t + 1) * TILE, :], (((1,), (1,)), ((), ())),
                            preferred_element_type=F32)
        e = e.reshape(CHIPS, 8, TILE)
        return jnp.concatenate([e[..., :BLK], e[..., BLK:]], axis=1)

    swaps = [net.group() for _ in range(PARTS)]
    shares = [net.group() for _ in range(PARTS)]
    for k in range(2):
        wait([whole[k]])
        it = ifull[k].reshape(BLK, INNER)

        @pl.when(c != k)
        def _(k=k, it=it):
            for part in range(PARTS):
                for t in range(per):
                    eoth[part, :, :, t * BLK:(t + 1) * BLK] = tile(it, part * per + t).astype(BF16)
                net.start(eoth.at[part], eland.at[part], other, swaps[part], counted=k == 0)

        @pl.when(c == k)
        def _(k=k, it=it):
            for part in range(PARTS):
                for t in range(per):
                    eown[part, :, :, t * BLK:(t + 1) * BLK] = tile(it, part * per + t)
            for part in range(PARTS):
                net.take(recv.at[swaps[part]], math.prod(eoth.shape[1:]) // UNIT)
                for d in range(CHIPS):
                    summed = eown[part, d] + eland[part, (d + 8) % CHIPS].astype(F32)
                    eown[part, d] = summed
                    ssend[part, d] = summed.astype(BF16)
                for i, (dx, dy) in enumerate(PLANE):
                    tx, ty = (x + dx) % NX, (y + dy) % NY
                    net.start(ssend.at[part, (tx * 4 + ty + 8 * c) % CHIPS], sland.at[part, i],
                              device(tx, ty, c, z), shares[part], 6, k == 0)
    net.drain()
    for k in range(PARTS):
        wait([shares[k]])
        total = eown[k, (chip + 8 * c) % CHIPS]
        for i in range(CHIPS - 1):
            total += sland[k, i].astype(F32)
        for t in range(per):
            at = (k * per + t) * TILE
            out[:, at:at + BLK] = total[0:8, t * BLK:(t + 1) * BLK]
            out[:, at + BLK:at + TILE] = total[8:16, t * BLK:(t + 1) * BLK]


def body(three_index, home_panels, panel_owner, block_row, block_column, block_count):
    anywhere = pl.BlockSpec(memory_space=pl.ANY)
    smem = pl.BlockSpec(memory_space=pltpu.SMEM)
    dma = pltpu.SemaphoreType.DMA
    vm = pltpu.VMEM
    pieces = [(n // 2, 16, BLK) for n in BLOCKS]
    packed = (PARTS, CHIPS, 16, ROWS // 2 // PARTS)
    out = pl.pallas_call(
        kernel,
        name="exchange",
        out_shape=jax.ShapeDtypeStruct((8, ROWS), F32),
        in_specs=[anywhere] * 6,
        out_specs=pl.BlockSpec(memory_space=vm),
        scratch_shapes=[
            vm((NZ, ROW_BLOCKS, BLK, BLK), BF16),
            pltpu.SMEM((32,), jnp.int32),
            vm((ROW_BLOCKS, BLK, BLK), BF16),
        ] + [
            vm((CHIPS,) + piece, BF16) for piece in pieces
        ] + [
            vm(piece, BF16) for piece in pieces
        ] + [
            vm((2,) + piece, BF16) for piece in pieces
        ] + [
            vm(three_index.shape, BF16),
            vm(three_index.shape, BF16),
            vm((2,) + block_row.shape, jnp.int32),
            vm(block_count.shape, jnp.int32),
            pltpu.SMEM((2,) + block_row.shape, jnp.int32),
            pltpu.SMEM((2,) + block_row.shape, jnp.int32),
            pltpu.SMEM((2,) + block_count.shape, jnp.int32),
            pltpu.SMEM((2, SLOTS), jnp.int32),
            pltpu.SMEM((2, ROW_BLOCKS), jnp.int32),
            vm((2, SLOTS + 1, 2 * BLK, BLK), F32),
            vm((ROWS, INNER), BF16),
            vm((ROW_BLOCKS, BLK, BLK), BF16),
            vm((2, NZ, 16, INNER), BF16),
            vm((2, NZ - 1, 16, INNER), BF16),
            vm((2, NZ, 16, INNER), BF16),
            vm(packed, F32),
            vm(packed, BF16),
            vm(packed, BF16),
            vm(packed, BF16),
            vm((PARTS, CHIPS - 1) + packed[2:], BF16),
            dma((PHASES + 3,)),
            dma((GROUPS,)),
            dma((9,)),
        ],
        compiler_params=pltpu.CompilerParams(collective_id=0, has_side_effects=True, vmem_limit_bytes=48 * 2**20),
    )(*[
        pltpu.with_memory_space_constraint(value, pltpu.HBM)
        for value in (panel_owner, home_panels.reshape(ROW_BLOCKS, BLK, BLK), three_index, block_row, block_column)
    ], block_count)
    return out.T


def solution(mesh):
    placed = (
        P("aux", "orb", None, None),
        P("aux", "orb", None),
        P(),
        P("aux", "orb", None),
        P("aux", "orb", None),
        P("aux", "orb"),
    )
    return jax.shard_map(
        body, mesh=mesh, in_specs=placed, out_specs=P("orb", "aux"), check_vma=False
    )
```

```python
import math

import jax
import jax.numpy as jnp
from jax import lax
from jax.experimental import pallas as pl
from jax.experimental.pallas import tpu as pltpu
from jax.sharding import PartitionSpec as P

MESH = pl.DeviceIdType.MESH
BF16 = jnp.bfloat16
F32 = jnp.float32
BLK = 128
NX, NY, NZ = 4, 4, 8
CHIPS = NX * NY
PLANE = [(2, 2), (2, 1), (2, 3), (1, 2), (3, 2), (2, 0), (0, 2), (1, 1), (1, 3), (3, 1), (3, 3), (1, 0), (3, 0), (0, 1), (0, 3)]
LINE = (4, 3, 5, 2, 6, 1, 7)
ROWS = 2560
SLOTS = 24
ROW_BLOCKS = ROWS // BLK
BLOCKS = [4, 4, 6, 6]
FIRST = [sum(BLOCKS[:p]) for p in range(4)]
INNER = 512
TILE = 256
TILES = ROWS // TILE
PARTS = 2
UNIT = 16 * BLK
GROUPS = 99
PHASES = 7


def here():
    a = lax.axis_index("aux")
    return a // 8, (a // 2) % 4, a % 2, lax.axis_index("orb")


def device(x, y, core, z):
    return ((x * 4 + y) * 2 + core, z)


class Copies:
    def __init__(self, send, recv, ruler):
        self.send, self.recv, self.ruler = send, recv, ruler
        self.used, self.phase, self.out, self.due = 0, 0, {}, {}

    def group(self):
        self.used += 1
        return self.used - 1

    def start(self, src, dst, target, group=None, phase=None, counted=True):
        group = self.group() if group is None else group
        phase = self.phase if phase is None else phase
        copy = pltpu.make_async_remote_copy(
            src_ref=src, dst_ref=dst, send_sem=self.send.at[phase], recv_sem=self.recv.at[group],
            device_id=target, device_id_type=MESH,
        )
        copy.start()
        size = math.prod(src.shape) // UNIT if counted else 0
        self.out[phase] = self.out.get(phase, 0) + size
        self.due[group] = self.due.get(group, 0) + size
        return group

    def take(self, sem, size):
        fits = [(a, r) for a in range(1, NZ + 1) for r in range(1, 9)
                if size % (a * r) == 0 and size // (a * r) <= ROW_BLOCKS]
        a, r = fits[0]
        ref = self.ruler.at[pl.ds(0, a), pl.ds(0, size // (a * r)), pl.ds(0, r * 16)]
        pltpu.make_async_copy(ref, ref, sem).wait()

    def wait(self, groups):
        for group in groups:
            self.take(self.recv.at[group], self.due.pop(group))

    def drain(self):
        for phase, size in self.out.items():
            self.take(self.send.at[phase], size)
        self.out = {}


def peers(x, y, c, z):
    return (
        [device((x + dx) % NX, (y + dy) % NY, c, z) for dx, dy in PLANE]
        + [device(x, y, c, (z + dz) % NZ) for dz in LINE]
        + [device(x, y, 1 - c, z)]
    )


def kernel(owner_h, home, tri, row, col, cnt, out,
           panel, owner, home_v, land0, land1, land2, land3, sel0, sel1, sel2, sel3, cand0, cand1, cand2, cand3, own_t, other_t, lists_v, cnt_v, row_s, col_s, cnt_s, prev, last, run, half,
           other_rows, ip, ip_land, ifull, eown, eoth, eland, ssend, sland, send, recv, local):
    land, sel, cand = (land0, land1, land2, land3), (sel0, sel1, sel2, sel3), (cand0, cand1, cand2, cand3)
    x, y, c, z = here()
    chip = x * 4 + y
    other = device(x, y, 1 - c, z)
    targets = peers(x, y, c, z)
    barrier = pltpu.get_barrier_semaphore()
    for target in targets:
        pl.semaphore_signal(barrier, inc=1, device_id=target, device_id_type=MESH)
    net = Copies(send, recv, panel)
    wait = net.wait

    def piece(p, j):
        n = BLOCKS[p] // 2
        return pl.ds(FIRST[p] + j // 8 * n, n), pl.ds(j % 8 * 16, 16)

    fetch = pltpu.make_async_copy(home, home_v, local.at[0])
    fetch.start()
    here_copies = [
        pltpu.make_async_copy(row, row_s.at[0], local.at[1]),
        pltpu.make_async_copy(col, col_s.at[0], local.at[2]),
        pltpu.make_async_copy(cnt, cnt_s.at[0], local.at[3]),
        pltpu.make_async_copy(tri, own_t, local.at[4]),
    ]
    own_list = pltpu.make_async_copy(owner_h, owner, local.at[8])
    own_list.start()
    for copy in here_copies[:3]:
        copy.start()
    own_list.wait()
    def look_up(u):
        if u == 0:
            for copy in here_copies[:3]:
                copy.wait()
        else:
            for copy in lists:
                copy.wait()
            to_smem = [
                pltpu.make_async_copy(lists_v.at[0], row_s.at[1], local.at[5]),
                pltpu.make_async_copy(lists_v.at[1], col_s.at[1], local.at[6]),
                pltpu.make_async_copy(cnt_v, cnt_s.at[1], local.at[7]),
            ]
            for copy in to_smem:
                copy.start()
            for copy in to_smem:
                copy.wait()

        @pl.loop(0, SLOTS)
        def _(s):
            mine = row_s[u, 0, 0, s]
            found = jnp.int32(SLOTS)
            for e in range(SLOTS - 1):
                same = jnp.logical_and(row_s[u, 0, 0, e] == mine, e < s)
                found = jnp.where(same, jnp.int32(e), found)
            prev[u, s] = found

        @pl.loop(0, ROW_BLOCKS)
        def _(t):
            found = jnp.int32(SLOTS)
            for e in range(SLOTS):
                same = jnp.logical_and(row_s[u, 0, 0, e] == t, e < cnt_s[u, 0, 0])
                found = jnp.where(same, jnp.int32(e), found)
            last[u, t] = found

        run[u, SLOTS] = jnp.zeros((2 * BLK, BLK), F32)

    fetch.wait()
    for p in range(4):
        land[p][chip] = home_v[piece(p, chip)]
    look_up(0)
    pl.semaphore_wait(barrier, len(targets))

    scatter = [net.group() for _ in range(4)]

    def deal(p):
        for dx, dy in PLANE:
            tx, ty = (x + dx) % NX, (y + dy) % NY
            net.start(home_v.at[piece(p, tx * 4 + ty)], land[p].at[chip], device(tx, ty, c, z), scatter[p])

    for p in (2, 0, 3, 1):
        deal(p)
    lists = [
        pltpu.make_async_remote_copy(
            src_ref=src, dst_ref=dst, send_sem=send.at[PHASES + i], recv_sem=recv.at[net.group()],
            device_id=other, device_id_type=MESH,
        )
        for i, (src, dst) in enumerate(((row, lists_v.at[0]), (col, lists_v.at[1]), (cnt, cnt_v)))
    ]
    for copy in lists:
        copy.start()
    here_copies[3].start()

    tri_copy = net.start(tri, other_t, other, None, 2)
    look_up(1)

    def choose(p):
        wait([scatter[p]])
        sel[p][...] = land[p][owner[1 - c] // 2]
        passed = net.start(sel[p], cand[p].at[1], other)
        cand[p][0] = land[p][owner[c] // 2]
        wait([passed])
        panel[(0,) + piece(p, chip)] = cand[p][(owner[c] + c) % 2]

    ring, plane = {}, {}

    def to_plane(p):
        choose(p)
        mine = panel.at[(0,) + piece(p, chip)]
        plane[p] = net.group()
        for dx, dy in PLANE:
            net.start(mine, mine, device((x + dx) % NX, (y + dy) % NY, c, z), plane[p])

    def step(p, k):
        for e in range(2):
            for sign in (1, -1):
                if k > (4 if (sign == 1) == (e == 0) else 3):
                    continue
                if k > 1:
                    wait([ring[p, k - 1, e, sign]])
                n = BLOCKS[p] // 2
                blocks = pl.ds(FIRST[p] + e * n, n)
                ring[p, k, e, sign] = net.start(
                    panel.at[-sign * (k - 1) % NZ, blocks], panel.at[-sign * k % NZ, blocks],
                    device(x, y, c, (z + sign + NZ) % NZ), None, 2)

    column, chunks, first, second, tail = {}, {}, {}, {}, net.group()
    uv = [(x, y), (y, x)]

    def to_column(p):
        choose(p)
        column[p] = net.group()
        for dz in LINE:
            net.start(panel.at[(0,) + piece(p, chip)], panel.at[(NZ - dz,) + piece(p, chip)],
                      device(x, y, c, (z + dz) % NZ), column[p])

    def block(p, h, u, v, skip, n):
        u, v = u % 4, v % 4
        return panel.at[(pl.ds(h * 4 + skip, n),) + piece(p, u * 4 + v if h == 0 else v * 4 + u)]

    def push(h, src, u, v, group=None):
        u, v = u % 4, v % 4
        return net.start(src, src, device(u, v, c, z) if h == 0 else device(v, u, c, z), group, 3)

    def begin(p):
        wait([column[p]])
        for h, (u, v) in enumerate(uv):
            src = block(p, h, u, v, 0, 4)
            first[p, h] = [push(h, src, u + 1, v), push(h, src, u + 3, v)]

    def spread(p, q, du):
        for h, (u, v) in enumerate(uv):
            src = block(p, h, u + du, v, 0, 4)
            chunks[p, q, h] = [push(h, src, u, v + 1), push(h, src, u, v + 3)]

    def pass_on(p):
        for h, (u, v) in enumerate(uv):
            up, down = first[p, h]
            second[p, h] = net.group()
            wait([up])
            push(h, block(p, h, u + 3, v, 0, 2), u + 1, v, second[p, h])
            wait([down])
            push(h, block(p, h, u + 1, v, 2, 2), u + 3, v, second[p, h])

    def relay(p, q, du):
        for h, (u, v) in enumerate(uv):
            up, down = chunks[p, q, h]
            wait([up])
            push(h, block(p, h, u + du, v + 3, 0, 2), u, v + 1, tail)
            wait([down])
            push(h, block(p, h, u + du, v + 1, 2, 2), u, v + 3, tail)

    def last_chunk(p):
        wait([second[p, h] for h in range(2)])
        spread(p, 3, 2)

    net.phase = 1
    to_column(2)
    to_plane(0)
    to_column(3)
    to_plane(1)
    begin(2)
    spread(2, 0, 0)
    wait([plane[0]])
    step(0, 1)
    begin(3)
    spread(3, 0, 0)
    wait([plane[1]])
    step(1, 1)
    pass_on(2)
    spread(2, 1, 3)
    spread(2, 2, 1)
    step(0, 2)
    relay(2, 0, 0)
    pass_on(3)
    spread(3, 1, 3)
    spread(3, 2, 1)
    step(1, 2)
    relay(3, 0, 0)
    last_chunk(2)
    relay(2, 1, 3)
    step(0, 3)
    relay(2, 2, 1)
    last_chunk(3)
    relay(3, 1, 3)
    step(1, 3)
    relay(3, 2, 1)
    relay(2, 3, 2)
    step(0, 4)
    relay(3, 3, 2)
    step(1, 4)
    net.phase = 5
    own_rows = [net.start(panel.at[0, pl.ds(0, FIRST[2])], other_rows.at[pl.ds(0, FIRST[2])], other)]
    wait([tail])
    rest = ROW_BLOCKS - FIRST[2]
    own_rows.append(net.start(panel.at[0, pl.ds(FIRST[2], rest)], other_rows.at[pl.ds(FIRST[2], rest)], other))
    for p in range(2):
        wait([ring[p, 3, 0, -1], ring[p, 3, 1, 1], ring[p, 4, 0, 1], ring[p, 4, 1, -1]])

    here_copies[3].wait()
    wait([tri_copy])
    for u, integrals in enumerate((own_t, other_t)):
        @pl.loop(0, SLOTS, step=8)
        def _(s0, u=u, integrals=integrals):
            products = []
            for i in range(8):
                b = col_s[u, 0, 0, s0 + i]
                rows = panel[(b // ROW_BLOCKS + NZ - z) % NZ, b % ROW_BLOCKS]
                t = integrals[:, s0 + i].reshape(2 * BLK, BLK)
                products.append(jnp.dot(t, rows, preferred_element_type=F32))
            for i in range(8):
                run[u, s0 + i] = products[i] + run[u, prev[u, s0 + i]]
    for u in range(2):
        @pl.loop(0, ROW_BLOCKS, step=4)
        def _(t, u=u):
            for i in range(4):
                total = run[u, last[u, t + i]].astype(BF16)
                at = pl.ds(pl.multiple_of((t + i) * BLK, BLK), BLK)
                for p in range(2):
                    half[at, pl.ds((2 * u + p) * BLK, BLK)] = total[p * BLK:(p + 1) * BLK]

    for q in range(2):
        if q == 1:
            wait(own_rows)
        rows = (panel[0] if q == 0 else other_rows[...]).reshape(ROWS, BLK)
        part = lax.dot_general(rows, half[...], (((0,), (0,)), ((), ())), preferred_element_type=F32)
        part = part.reshape(CHIPS // 2, 2, 8, INNER)
        for g in range(2):
            ip[g, q * 4:(q + 1) * 4] = part[:, g].reshape(4, 16, INNER).astype(BF16)

    shares, whole = [net.group() for _ in range(2)], [net.group() for _ in range(2)]
    for k in range(2):
        for dz in LINE:
            to = (z + dz) % NZ
            net.start(ip.at[k, to], ip_land.at[k, dz - 1], device(x, y, c, to), shares[k], 4)
    for k in range(2):
        wait([shares[k]])
        total = ip[k, z].astype(F32)
        for dz in range(1, NZ):
            total += ip_land[k, dz - 1].astype(F32)
        ifull[k, z] = total.astype(BF16)
        mine = ifull.at[k, z]
        for dz in LINE:
            net.start(mine, mine, device(x, y, c, (z + dz) % NZ), whole[k], 4)

    per = TILES // PARTS

    def tile(it, t):
        e = lax.dot_general(it, half[t * TILE:(t + 1) * TILE, :], (((1,), (1,)), ((), ())),
                            preferred_element_type=F32)
        e = e.reshape(CHIPS, 8, TILE)
        return jnp.concatenate([e[..., :BLK], e[..., BLK:]], axis=1)

    swaps = [net.group() for _ in range(PARTS)]
    shares = [net.group() for _ in range(PARTS)]
    for k in range(2):
        wait([whole[k]])
        it = ifull[k].reshape(BLK, INNER)

        @pl.when(c != k)
        def _(k=k, it=it):
            for part in range(PARTS):
                for t in range(per):
                    eoth[part, :, :, t * BLK:(t + 1) * BLK] = tile(it, part * per + t).astype(BF16)
                net.start(eoth.at[part], eland.at[part], other, swaps[part], counted=k == 0)

        @pl.when(c == k)
        def _(k=k, it=it):
            for part in range(PARTS):
                for t in range(per):
                    eown[part, :, :, t * BLK:(t + 1) * BLK] = tile(it, part * per + t)
            for part in range(PARTS):
                net.take(recv.at[swaps[part]], math.prod(eoth.shape[1:]) // UNIT)
                for d in range(CHIPS):
                    summed = eown[part, d] + eland[part, (d + 8) % CHIPS].astype(F32)
                    eown[part, d] = summed
                    ssend[part, d] = summed.astype(BF16)
                for i, (dx, dy) in enumerate(PLANE):
                    tx, ty = (x + dx) % NX, (y + dy) % NY
                    net.start(ssend.at[part, (tx * 4 + ty + 8 * c) % CHIPS], sland.at[part, i],
                              device(tx, ty, c, z), shares[part], 6, k == 0)
    net.drain()
    for k in range(PARTS):
        wait([shares[k]])
        total = eown[k, (chip + 8 * c) % CHIPS]
        for i in range(CHIPS - 1):
            total += sland[k, i].astype(F32)
        for t in range(per):
            at = (k * per + t) * TILE
            out[:, at:at + BLK] = total[0:8, t * BLK:(t + 1) * BLK]
            out[:, at + BLK:at + TILE] = total[8:16, t * BLK:(t + 1) * BLK]


def body(three_index, home_panels, panel_owner, block_row, block_column, block_count):
    anywhere = pl.BlockSpec(memory_space=pl.ANY)
    smem = pl.BlockSpec(memory_space=pltpu.SMEM)
    dma = pltpu.SemaphoreType.DMA
    vm = pltpu.VMEM
    pieces = [(n // 2, 16, BLK) for n in BLOCKS]
    packed = (PARTS, CHIPS, 16, ROWS // 2 // PARTS)
    out = pl.pallas_call(
        kernel,
        name="exchange",
        out_shape=jax.ShapeDtypeStruct((8, ROWS), F32),
        in_specs=[anywhere] * 6,
        out_specs=pl.BlockSpec(memory_space=vm),
        scratch_shapes=[
            vm((NZ, ROW_BLOCKS, BLK, BLK), BF16),
            pltpu.SMEM((32,), jnp.int32),
            vm((ROW_BLOCKS, BLK, BLK), BF16),
        ] + [
            vm((CHIPS,) + piece, BF16) for piece in pieces
        ] + [
            vm(piece, BF16) for piece in pieces
        ] + [
            vm((2,) + piece, BF16) for piece in pieces
        ] + [
            vm(three_index.shape, BF16),
            vm(three_index.shape, BF16),
            vm((2,) + block_row.shape, jnp.int32),
            vm(block_count.shape, jnp.int32),
            pltpu.SMEM((2,) + block_row.shape, jnp.int32),
            pltpu.SMEM((2,) + block_row.shape, jnp.int32),
            pltpu.SMEM((2,) + block_count.shape, jnp.int32),
            pltpu.SMEM((2, SLOTS), jnp.int32),
            pltpu.SMEM((2, ROW_BLOCKS), jnp.int32),
            vm((2, SLOTS + 1, 2 * BLK, BLK), F32),
            vm((ROWS, INNER), BF16),
            vm((ROW_BLOCKS, BLK, BLK), BF16),
            vm((2, NZ, 16, INNER), BF16),
            vm((2, NZ - 1, 16, INNER), BF16),
            vm((2, NZ, 16, INNER), BF16),
            vm(packed, F32),
            vm(packed, BF16),
            vm(packed, BF16),
            vm(packed, BF16),
            vm((PARTS, CHIPS - 1) + packed[2:], BF16),
            dma((PHASES + 3,)),
            dma((GROUPS,)),
            dma((9,)),
        ],
        compiler_params=pltpu.CompilerParams(collective_id=0, has_side_effects=True, vmem_limit_bytes=48 * 2**20),
    )(*[
        pltpu.with_memory_space_constraint(value, pltpu.HBM)
        for value in (panel_owner, home_panels.reshape(ROW_BLOCKS, BLK, BLK), three_index, block_row, block_column)
    ], block_count)
    return out.T


def solution(mesh):
    placed = (
        P("aux", "orb", None, None),
        P("aux", "orb", None),
        P(),
        P("aux", "orb", None),
        P("aux", "orb", None),
        P("aux", "orb"),
    )
    return jax.shard_map(
        body, mesh=mesh, in_specs=placed, out_specs=P("orb", "aux"), check_vma=False
    )
```
